32 devices in a mesh: dp: 4 (over z), gx: 2 (over x), gy: 4 (over y, core).
Axes of the slice: x: 2, y: 2, z: 4, core: 2. Of those that a mesh axis runs over, the one named last changes fastest.
Arguments:
- fields: bfloat16 [4, 20, 32, 16384], P('dp', None, None, ('gx', 'gy')), may hold values from -6 to 6
- cotangent: bfloat16 [4, 20, 32, 16384], P('dp', None, None, ('gx', 'gy')), may hold values from -6 to 6
- mix_weight: bfloat16 [20, 20], replicated, may hold values from -1.25 to 1.25
- spectral_weight: bfloat16 [288, 2, 20, 20], P(('gx', 'gy')), may hold values from -1 to 1
Outputs:
- output: bfloat16 [4, 20, 32, 16384], P('dp', None, None, ('gx', 'gy'))
- spectral_grad: float32 [288, 2, 20, 20], P(('gx', 'gy'))
- mixing_grad: float32 [20, 20], replicated
The draws below stay inside these ranges and needn't reach their ends.
All inputs are finite; a program needn't handle non-finite values.
Results may differ from the reference program's by a relative error of at most 0.0031.
Values may be sent and summed in bfloat16 or wider, within the bound.
No kernel may reach another device: no remote copies, remote signals or barrier semaphores. Data moves between devices by JAX's collectives and lax.ppermute only.
A program may use at most 128 MiB of HBM per device.

```python
import math
import jax
import jax.numpy as jnp
from jax import lax

C = 20
NX = 128
NY = 128
KX = 24
KY = 12
P_SIZE = 32
MODES = 288
CELLS = 16384
SAMPLES = 4


def block_scale(stream_key, extent, pieces, smallest, largest):
    def one(position, parts):
        draws = jax.random.uniform(jax.random.fold_in(jax.random.fold_in(stream_key, 6), position), (parts,), jnp.float32, smallest / len(pieces), largest / len(pieces))
        return jnp.repeat(jnp.exp(draws), extent[position] // parts).reshape((-1,) + (1,) * (len(extent) - position - 1))

    factor_of = one(*pieces[0])
    for cut in pieces[1:]:
        factor_of = factor_of * one(*cut)
    return factor_of


def normal_values(rng, extent, width, limit, pieces=(), kind=jnp.bfloat16):
    drawn = width * jax.random.normal(rng, extent, jnp.float32)
    if pieces:
        drawn = drawn * block_scale(rng, extent, pieces, -0.22, 0.18)
    return jnp.clip(drawn, -limit, limit).astype(kind)


def setup_inputs(seed: int = 0) -> dict:
    keys = jax.random.split(jax.random.key(seed), 5)
    fields = normal_values(keys[0], (SAMPLES, C, P_SIZE, CELLS), 1.0, 6.0, ((0, 4), (3, 8)))
    cotangent = normal_values(keys[1], (SAMPLES, C, P_SIZE, CELLS), 1.0, 6.0, ((0, 4), (3, 8)))
    mix_weight = normal_values(keys[2], (C, C), C ** -0.5, 1.25)
    spectral_weight = normal_values(keys[3], (MODES, 2, C, C), (2 * C) ** -0.5, 1.0, ((0, 8),))
    return {"fields": fields, "cotangent": cotangent, "mix_weight": mix_weight, "spectral_weight": spectral_weight}


HI = lax.Precision.HIGHEST

def gelu_value(h):
    k = math.sqrt(2.0 / math.pi)
    t = jnp.tanh(k * (h + 0.044715 * h * h * h))
    return 0.5 * h * (1.0 + t)

def gelu_slope(h):
    k = math.sqrt(2.0 / math.pi)
    t = jnp.tanh(k * (h + 0.044715 * h * h * h))
    return 0.5 * (1.0 + t) + 0.5 * h * (1.0 - t * t) * k * (1.0 + 3.0 * 0.044715 * h * h)

def axis_table(waves, n):
    cells = jnp.arange(n, dtype=jnp.int32)
    angle = 2.0 * math.pi / n * (waves[:, None] * cells[None, :] % n).astype(jnp.float32)
    return (jnp.cos(angle), jnp.sin(angle))

def tables():
    index = jnp.arange(KX, dtype=jnp.int32)
    waves_x = jnp.where(index < KX // 2, index, NX - KX + index).astype(jnp.int32)
    cos_x, sin_x = axis_table(waves_x, NX)
    cos_y, sin_y = axis_table(jnp.arange(KY, dtype=jnp.int32), NY)
    return (cos_x, sin_x, cos_y, sin_y)

def forward_dft(data, scale):
    cos_x, sin_x, cos_y, sin_y = tables()
    a_re = jnp.einsum('cpxy,ky->cpxk', data, cos_y, precision=HI)
    a_im = -jnp.einsum('cpxy,ky->cpxk', data, sin_y, precision=HI)
    s_re = jnp.einsum('cpxk,jx->jkcp', a_re, cos_x, precision=HI) + jnp.einsum('cpxk,jx->jkcp', a_im, sin_x, precision=HI)
    s_im = jnp.einsum('cpxk,jx->jkcp', a_im, cos_x, precision=HI) - jnp.einsum('cpxk,jx->jkcp', a_re, sin_x, precision=HI)
    chans, planes = (data.shape[0], data.shape[1])
    return scale * jnp.stack([s_re.reshape(MODES, chans, planes), s_im.reshape(MODES, chans, planes)], axis=1)

def inverse_dft(vals, scale):
    cos_x, sin_x, cos_y, sin_y = tables()
    chans, planes = (vals.shape[2], vals.shape[3])
    v_re = vals[:, 0].reshape(KX, KY, chans, planes)
    v_im = vals[:, 1].reshape(KX, KY, chans, planes)
    b_re = jnp.einsum('jkdp,jx->dpxk', v_re, cos_x, precision=HI) - jnp.einsum('jkdp,jx->dpxk', v_im, sin_x, precision=HI)
    b_im = jnp.einsum('jkdp,jx->dpxk', v_re, sin_x, precision=HI) + jnp.einsum('jkdp,jx->dpxk', v_im, cos_x, precision=HI)
    return scale * (jnp.einsum('dpxk,ky->dpxy', b_re, cos_y, precision=HI) - jnp.einsum('dpxk,ky->dpxy', b_im, sin_y, precision=HI))

def spectral_mix(spec, weight):
    w = weight.astype(jnp.float32)
    v_re = jnp.einsum('mcp,mcd->mdp', spec[:, 0], w[:, 0], precision=HI) - jnp.einsum('mcp,mcd->mdp', spec[:, 1], w[:, 1], precision=HI)
    v_im = jnp.einsum('mcp,mcd->mdp', spec[:, 0], w[:, 1], precision=HI) + jnp.einsum('mcp,mcd->mdp', spec[:, 1], w[:, 0], precision=HI)
    return jnp.stack([v_re, v_im], axis=1)

def grads_of(spec, gspec):
    g_re = jnp.einsum('mcp,mdp->mcd', spec[:, 0], gspec[:, 0], precision=HI) + jnp.einsum('mcp,mdp->mcd', spec[:, 1], gspec[:, 1], precision=HI)
    g_im = jnp.einsum('mcp,mdp->mcd', spec[:, 0], gspec[:, 1], precision=HI) - jnp.einsum('mcp,mdp->mcd', spec[:, 1], gspec[:, 0], precision=HI)
    return jnp.stack([g_re, g_im], axis=1)

def reference(fields, cotangent, mix_weight, spectral_weight):
    norm_in = 1.0 / math.sqrt(NX * NY)
    norm_out = 1.0 / math.sqrt(MODES)
    mixing = mix_weight.astype(jnp.float32)

    def one_sample(pair):
        chans, planes = (pair[0].shape[0], pair[0].shape[1])
        field = pair[0].astype(jnp.float32).reshape(chans, planes, NX, NY)
        grad_out = pair[1].astype(jnp.float32).reshape(chans, planes, NX, NY)
        spec = forward_dft(field, norm_in)
        vals = spectral_mix(spec, spectral_weight)
        branch = inverse_dft(vals, norm_out)
        pre = branch + jnp.einsum('cpxy,cd->dpxy', field, mixing, precision=HI)
        result = gelu_value(pre).astype(jnp.bfloat16).reshape(chans, planes, NX * NY)
        back = (grad_out * gelu_slope(pre)).astype(jnp.bfloat16).astype(jnp.float32)
        gspec = forward_dft(back, norm_out)
        spec_grad = grads_of(spec, gspec)
        mix_grad = jnp.einsum('cpxy,dpxy->cd', field, back, precision=HI)
        return (result, spec_grad, mix_grad)
    output, spec_grads, mix_grads = lax.map(one_sample, (fields, cotangent))
    spectral_grad = lax.optimization_barrier(jnp.sum(spec_grads, axis=0)) / math.sqrt(SAMPLES * P_SIZE)
    mixing_grad = lax.optimization_barrier(jnp.sum(mix_grads, axis=0)) / math.sqrt(SAMPLES * P_SIZE * NX * NY)
    return (output, spectral_grad, mixing_grad)
```

```python
import functools
import math

import jax
import jax.numpy as jnp
import ml_dtypes
import numpy as np
from jax import lax
from jax.experimental import pallas as pl
from jax.experimental.pallas import tpu as pltpu
from jax.sharding import PartitionSpec as P

NX = 128
NY = 128
KX = 24
KY = 12
MODES = 288
C = 20
PL = 32
CP = C * PL
CR = 24
SCALE = 1.6656925
GROUP = ("gx", "gy")
BF = jnp.bfloat16
F32 = jnp.float32


def round_up(n, k):
    return -(-n // k) * k


def table(groups):
    per = MODES // groups
    rows = round_up(2 * per, 8)
    index = np.arange(KX)
    waves_x = np.where(index < KX // 2, index, NX - KX + index)
    kx = np.repeat(waves_x, KY)
    ky = np.tile(np.arange(KY), KX)
    x = np.arange(NX * NY) // NY
    y = np.arange(NX * NY) % NY
    turn = (kx[:, None] * x[None] + ky[:, None] * y[None]) % 128
    wheel = 2.0 * np.pi * np.arange(128) / 128
    both = np.stack([(SCALE * np.cos(wheel))[turn], (-SCALE * np.sin(wheel))[turn]], 0)
    both = both.reshape(2, groups, per, -1).transpose(1, 0, 2, 3).reshape(groups, 2 * per, -1)
    full = np.zeros((groups, rows, NX * NY), np.float32)
    full[:, : 2 * per] = both
    full = full.reshape(groups * rows, groups, -1).transpose(1, 0, 2)
    return full.astype(ml_dtypes.bfloat16)


def selectors(groups):
    per = MODES // groups
    rows = round_up(2 * per, 8)
    re, im = np.arange(per), per + np.arange(per)
    spread = np.zeros((rows, 256), np.float32)
    spread[re, re] = 1
    spread[im, im] = 1
    spread[im, 128 + re] = -1
    spread[re, 128 + im] = 1
    weights = np.zeros((per, 128), np.float32)
    weights[re, re] = 1
    weights[re, im] = 1
    collect = np.zeros((rows, 128), np.float32)
    collect[re, re] = 1
    collect[im, im] = 1
    fold = np.zeros((rows, 256), np.float32)
    fold[re, re] = 1
    fold[re, im] = 1
    fold[im, 128 + re] = 1
    fold[im, 128 + im] = 1
    cast = lambda a: a.astype(ml_dtypes.bfloat16)
    return (
        cast(np.concatenate([spread, spread], 0)),
        cast(weights),
        cast(np.concatenate([collect, collect], 1)),
        cast(np.concatenate([fold, fold], 1)),
    )


def expander():
    e = np.zeros((CP, 128), np.float32)
    e[np.arange(CP), np.arange(CP) // PL] = 1
    return e.astype(ml_dtypes.bfloat16)


def dot(a, b, ca, cb):
    return lax.dot_general(a, b, (((ca,), (cb,)), ((), ())), preferred_element_type=F32)


def encode(v):
    return ((v * jnp.abs(v)) * (v * v)).astype(BF)


def decode(y):
    y = y.astype(F32)
    z = lax.rsqrt(jnp.maximum(jnp.abs(y), 1e-36))
    return ((y * z) * z) * lax.rsqrt(z)


def split(v):
    hi = v.astype(BF)
    return hi, (v - hi.astype(F32)).astype(BF)


def first_kernel(groups, rows, steps, gid_ref, f_ref, t_ref, o_ref, acc_ref):
    step = pl.program_id(0)
    part = dot(t_ref[0], f_ref[...], 1, 1)

    @pl.when(step == 0)
    def _():
        acc_ref[...] = part

    @pl.when(step > 0)
    def _():
        acc_ref[...] += part

    @pl.when(step == steps - 1)
    def _():
        for g in range(groups):
            o_ref[g] = encode(acc_ref[g * rows : (g + 1) * rows, :])


def mix_kernel(groups, rows, r_ref, w_ref, spread_ref, wsel_ref, collect_ref, v_ref, s_ref, wa_ref, wb_ref, vals_ref):
    total = decode(r_ref[0])
    for g in range(1, groups):
        total = total + decode(r_ref[g])
    total = total * (1.0 / (SCALE * math.sqrt(NX * NY)))
    hi, lo = split(total)
    both = jnp.concatenate([hi.astype(F32), lo.astype(F32)], 0).astype(BF)
    s_ref[0, 0:CP, :] = dot(both, spread_ref[:, 0:128], 0, 0)
    s_ref[1, 0:CP, :] = dot(both, spread_ref[:, 128:256], 0, 0)
    s_ref[:, CP:, :] = jnp.zeros((2, CR * PL - CP, 128), F32)
    w = w_ref[...]
    wa_ref[...] = dot(w[:, : C * C], wsel_ref[...], 0, 0)
    wb_ref[...] = dot(w[:, C * C :], wsel_ref[...], 0, 0)

    def some(block, _):
        base = block * 4
        acc = [None] * 4
        for c in range(C):
            s = s_ref[0, c * PL : (c + 1) * PL, :]
            t = s_ref[1, c * PL : (c + 1) * PL, :]
            for k in range(4):
                row = c * C + base + k
                term = s * wa_ref[pl.ds(row, 1), :] + t * wb_ref[pl.ds(row, 1), :]
                acc[k] = term if acc[k] is None else acc[k] + term
        for k in range(4):
            vals_ref[pl.ds(pl.multiple_of((base + k) * PL, PL), PL), :] = acc[k]
        return 0

    lax.fori_loop(0, C // 4, some, 0)
    vals = vals_ref[...] * (1.0 / (SCALE * math.sqrt(MODES)))
    hi, lo = split(vals)
    v_ref[...] = dot(collect_ref[...], jnp.concatenate([hi, lo], 1), 1, 1).astype(BF)


def gelu_both(h):
    k = math.sqrt(2.0 / math.pi)
    h2 = h * h
    t = jnp.tanh(h * (k + (k * 0.044715) * h2))
    half = 0.5 + 0.5 * t
    slope = half + (h * (half * (1.0 - t))) * (k + (3.0 * 0.044715 * k) * h2)
    return h * half, slope


def same_plane(n):
    i = lax.broadcasted_iota(jnp.int32, (n, n), 0)
    j = lax.broadcasted_iota(jnp.int32, (n, n), 1)
    return lax.rem(i, PL) == lax.rem(j, PL)


def main_kernel(
    groups, rows, steps, gid_ref, f_ref, cot_ref, t_ref, v_ref, mix_ref, e_ref,
    out_ref, o_ref, a_ref, m_ref, acc_ref, accm_ref,
):
    step = pl.program_id(0)

    @pl.when(step == 0)
    def _():
        a_ref[...] = jnp.transpose(v_ref[...].astype(F32)).astype(BF)
        e = e_ref[:, 0:C]
        u = dot(e, mix_ref[...], 1, 1).astype(BF)
        m = dot(u, e, 1, 1)
        m_ref[...] = jnp.where(same_plane(CP), m, 0.0).astype(BF)

    t = t_ref[0]
    f = f_ref[...]
    pre = dot(a_ref[...], t, 1, 0) + dot(m_ref[...], f, 1, 0)
    value, slope = gelu_both(pre)
    out_ref[...] = value.astype(BF)
    back = (cot_ref[...].astype(F32) * slope).astype(BF)
    part = dot(t, back, 1, 1)
    partm = dot(f, back, 1, 1)

    @pl.when(step == 0)
    def _():
        acc_ref[...] = part
        accm_ref[...] = partm

    @pl.when(step > 0)
    def _():
        acc_ref[...] += part
        accm_ref[...] += partm

    @pl.when(step == steps - 1)
    def _():
        kept = jnp.where(same_plane(CP), accm_ref[...], 0.0)
        kept = jnp.sum(kept.reshape(C, PL, CP), axis=1)
        kept = jnp.concatenate([kept, jnp.zeros((CR - C, CP), F32)], 0)
        hi, lo = split(kept)
        y = dot(hi, e_ref[...], 1, 0) + dot(lo, e_ref[...], 1, 0)
        yh = y.astype(BF).astype(F32)
        y = yh + pltpu.roll(y - yh, 64, 1)
        extra = jnp.concatenate([y[0:8], y[8:16], y[16:24], jnp.zeros((8, CP - 384), F32)], 1).astype(BF)
        extra = extra.astype(F32)
        for g in range(groups):
            v = acc_ref[g * rows : (g + 1) * rows, :]
            coded = (v * jnp.abs(v)) * (v * v)
            o_ref[g] = jnp.concatenate([coded, extra], 0).astype(BF)


def grad_kernel(groups, rows, r_ref, s_ref, spread_ref, fold_ref, o_ref, g_ref, p_ref):
    total = None
    extra = None
    for g in range(groups):
        block = r_ref[g].astype(F32)
        y = block[0:rows]
        z = lax.rsqrt(jnp.maximum(jnp.abs(y), 1e-36))
        y = ((y * z) * z) * lax.rsqrt(z)
        total = y if total is None else total + y
        x = block[rows : rows + 8]
        extra = x if extra is None else extra + x
    total = total * (1.0 / (SCALE * math.sqrt(MODES)))
    hi, lo = split(total)
    both = jnp.concatenate([hi.astype(F32), lo.astype(F32)], 0).astype(BF)
    g_ref[...] = dot(both, spread_ref[:, 0:128], 0, 0)

    def some(block, _):
        base = block * 4
        one = [jnp.zeros((CR, 128), F32)] * 4
        two = [jnp.zeros((CR, 128), F32)] * 4
        for p in range(PL):
            s = s_ref[0, pl.ds(p, CR, stride=PL), :]
            t = s_ref[1, pl.ds(p, CR, stride=PL), :]
            for k in range(4):
                g = g_ref[pl.ds((base + k) * PL + p, 1), :]
                one[k] = one[k] + s * g
                two[k] = two[k] + t * g
        for k in range(4):
            at = pl.multiple_of((base + k) * CR, CR)
            p_ref[pl.ds(at, CR), 0:128] = one[k]
            p_ref[pl.ds(at, CR), 128:256] = two[k]
        return 0

    lax.fori_loop(0, C // 4, some, 0)
    hi, lo = split(p_ref[...])
    grads = dot(fold_ref[...], jnp.concatenate([hi, lo], 1), 1, 1)
    grads = jnp.concatenate([grads, jnp.zeros((rows, 512 - C * CR), F32)], 1)
    extra = extra[:, 0:512]
    extra = extra + pltpu.roll(extra, 512 - 64, 1)
    all_rows = jnp.concatenate([grads, extra], 0)
    o_ref[...] = (all_rows * jnp.abs(all_rows)) * (all_rows * all_rows)


def compiler_params(mib):
    return pltpu.CompilerParams(vmem_limit_bytes=mib * 2**20)


def local(tables, consts, fields, cotangent, mix_weight, spectral_weight):
    spread, wsel, collect, fold = consts
    cells = fields.shape[3]
    groups = lax.axis_size("gx") * lax.axis_size("gy")
    samples = lax.axis_size("dp")
    per = MODES // groups
    rows = round_up(2 * per, 8)
    flat = fields.reshape(CP, cells)
    cot = cotangent.reshape(CP, cells)
    gid = (lax.axis_index("gx") * lax.axis_size("gy") + lax.axis_index("gy")).astype(jnp.int32).reshape(1)
    width = min(512, cells)
    steps = cells // width
    whole = lambda shape: pl.BlockSpec(shape, lambda *_: (0,) * len(shape))
    cells_spec = pl.BlockSpec((CP, width), lambda i, gid: (0, i))
    table_spec = pl.BlockSpec((1, groups * rows, width), lambda i, gid: (gid[0], 0, i))

    sent = pl.pallas_call(
        functools.partial(first_kernel, groups, rows, steps),
        grid_spec=pltpu.PrefetchScalarGridSpec(
            num_scalar_prefetch=1,
            grid=(steps,),
            in_specs=[cells_spec, table_spec],
            out_specs=whole((groups, rows, CP)),
            scratch_shapes=[pltpu.VMEM((groups * rows, CP), F32)],
        ),
        out_shape=jax.ShapeDtypeStruct((groups, rows, CP), BF),
        compiler_params=compiler_params(32),
        name="spectrum_parts",
    )(gid, flat, tables)
    got = lax.all_to_all(sent, GROUP, 0, 0, tiled=True)

    weights = spectral_weight.reshape(per, 2 * C * C)
    vals, spec = pl.pallas_call(
        functools.partial(mix_kernel, groups, rows),
        out_shape=(jax.ShapeDtypeStruct((rows, CP), BF), jax.ShapeDtypeStruct((2, CR * PL, 128), F32)),
        scratch_shapes=[pltpu.VMEM((C * C, 128), F32), pltpu.VMEM((C * C, 128), F32), pltpu.VMEM((CP, 128), F32)],
        compiler_params=compiler_params(32),
        name="mode_mixing",
    )(got, weights, spread, wsel, collect)
    all_vals = lax.all_gather(vals, GROUP, axis=0, tiled=True)

    output, sent = pl.pallas_call(
        functools.partial(main_kernel, groups, rows, steps),
        grid_spec=pltpu.PrefetchScalarGridSpec(
            num_scalar_prefetch=1,
            grid=(steps,),
            in_specs=[
                cells_spec,
                cells_spec,
                table_spec,
                whole((groups * rows, CP)),
                whole((C, C)),
                whole((CP, 128)),
            ],
            out_specs=[cells_spec, whole((groups, rows + 8, CP))],
            scratch_shapes=[
                pltpu.VMEM((CP, groups * rows), BF),
                pltpu.VMEM((CP, CP), BF),
                pltpu.VMEM((groups * rows, CP), F32),
                pltpu.VMEM((CP, CP), F32),
            ],
        ),
        out_shape=(
            jax.ShapeDtypeStruct((CP, cells), BF),
            jax.ShapeDtypeStruct((groups, rows + 8, CP), BF),
        ),
        compiler_params=compiler_params(48),
        name="cells",
    )(gid, flat, cot, tables, all_vals, mix_weight, expander())
    got = lax.all_to_all(sent, GROUP, 0, 0, tiled=True)

    coded = pl.pallas_call(
        functools.partial(grad_kernel, groups, rows),
        out_shape=jax.ShapeDtypeStruct((rows + 8, 512), F32),
        scratch_shapes=[pltpu.VMEM((CP, 128), F32), pltpu.VMEM((C * CR, 256), F32)],
        compiler_params=compiler_params(32),
        name="mode_grads",
    )(got, spec, spread, fold)
    coded = coded.astype(BF)
    total = decode(coded)
    for k in range(1, samples):
        total = total + decode(lax.ppermute(coded, "dp", [(i, (i + k) % samples) for i in range(samples)]))

    grads = total[: 2 * per, : C * CR].reshape(2, per, C, CR)[..., :C]
    spectral_grad = jnp.transpose(grads, (1, 0, 3, 2)) * (1.0 / math.sqrt(samples * PL))
    extra = total[rows:, :384].reshape(8, 3, 128)[:, :, :C]
    mixing = jnp.transpose(extra, (1, 0, 2)).reshape(24, C)[:C]
    mixing_grad = mixing * (1.0 / math.sqrt(samples * PL * NX * NY))
    return (output.reshape(1, C, PL, cells), spectral_grad, mixing_grad)


def solution(mesh):
    groups = mesh.shape["gx"] * mesh.shape["gy"]
    body = functools.partial(local, table(groups), selectors(groups))
    return jax.shard_map(
        body,
        mesh=mesh,
        in_specs=(
            P("dp", None, None, GROUP),
            P("dp", None, None, GROUP),
            P(),
            P(GROUP, None, None, None),
        ),
        out_specs=(P("dp", None, None, GROUP), P(GROUP, None, None, None), P()),
        check_vma=False,
    )
```

```python
import functools
import math

import jax
import jax.numpy as jnp
import ml_dtypes
import numpy as np
from jax import lax
from jax.experimental import pallas as pl
from jax.experimental.pallas import tpu as pltpu
from jax.sharding import PartitionSpec as P

NX = 128
NY = 128
KX = 24
KY = 12
MODES = 288
C = 20
PL = 32
CP = C * PL
HP = 16
HALF = C * HP
CR = 24
SCALE = 1.6656925
GROUP = ("gx", "gy")
BF = jnp.bfloat16
F32 = jnp.float32


def round_up(n, k):
    return -(-n // k) * k


def table(groups):
    per = MODES // groups
    rows = round_up(2 * per, 8)
    index = np.arange(KX)
    waves_x = np.where(index < KX // 2, index, NX - KX + index)
    kx = np.repeat(waves_x, KY)
    ky = np.tile(np.arange(KY), KX)
    x = np.arange(NX * NY) // NY
    y = np.arange(NX * NY) % NY
    turn = (kx[:, None] * x[None] + ky[:, None] * y[None]) % 128
    wheel = 2.0 * np.pi * np.arange(128) / 128
    both = np.stack([(SCALE * np.cos(wheel))[turn], (-SCALE * np.sin(wheel))[turn]], 0)
    both = both.reshape(2, groups, per, -1).transpose(1, 0, 2, 3).reshape(groups, 2 * per, -1)
    full = np.zeros((groups, rows, NX * NY), np.float32)
    full[:, : 2 * per] = both
    full = full.reshape(groups * rows, groups, -1).transpose(1, 0, 2)
    return full.astype(ml_dtypes.bfloat16)


def selectors(groups):
    per = MODES // groups
    rows = round_up(2 * per, 8)
    re, im = np.arange(per), per + np.arange(per)
    spread = np.zeros((rows, 256), np.float32)
    spread[re, re] = 1
    spread[im, im] = 1
    spread[im, 128 + re] = -1
    spread[re, 128 + im] = 1
    weights = np.zeros((per, 128), np.float32)
    weights[re, re] = 1
    weights[re, im] = 1
    collect = np.zeros((rows, 128), np.float32)
    collect[re, re] = 1
    collect[im, im] = 1
    fold = np.zeros((rows, 256), np.float32)
    fold[re, re] = 1
    fold[re, im] = 1
    fold[im, 128 + re] = 1
    fold[im, 128 + im] = 1
    cast = lambda a: a.astype(ml_dtypes.bfloat16)
    return (
        cast(np.concatenate([spread, spread], 0)),
        cast(weights),
        cast(np.concatenate([collect, collect], 1)),
        cast(np.concatenate([fold, fold], 1)),
    )


def dot(a, b, ca, cb):
    return lax.dot_general(a, b, (((ca,), (cb,)), ((), ())), preferred_element_type=F32)


def encode(v):
    return ((v * jnp.abs(v)) * (v * v)).astype(BF)


def decode(y):
    y = y.astype(F32)
    z = lax.rsqrt(jnp.maximum(jnp.abs(y), 1e-36))
    return ((y * z) * z) * lax.rsqrt(z)


def split(v):
    hi = v.astype(BF)
    return hi, (v - hi.astype(F32)).astype(BF)


def chunk_copies(pairs, parts, sem):
    copies = []
    for j in range(parts):
        copies.append([])
        for k, (source, target) in enumerate(pairs):
            width = target.shape[-1] // parts
            index = (slice(None),) * (len(target.shape) - 1) + (pl.ds(j * width, width),)
            copies[j].append(pltpu.make_async_copy(source.at[index], target.at[index], sem.at[k, j]))
    return copies


def start_chunk(copies, j):
    if j < len(copies):
        for copy in copies[j]:
            copy.start()


def first_kernel(groups, rows, parts, gid_ref, f_hbm, t_hbm, o_hbm, f_ref, t_ref, acc_ref, o_ref, sem, o_sem):
    gid = gid_ref[0]
    width = f_ref.shape[1] // parts
    copies = chunk_copies([(f_hbm, f_ref), (t_hbm.at[gid], t_ref)], parts, sem)
    for j in range(parts):
        start_chunk(copies, j)
    for j in range(parts):
        at = slice(j * width, (j + 1) * width)
        for copy in copies[j]:
            copy.wait()
        part = dot(t_ref[:, at], f_ref[:, at], 1, 1)
        if j == 0:
            acc_ref[...] = part
        elif j < parts - 1:
            acc_ref[...] += part
    sent = acc_ref[...] + part if parts > 1 else part
    out = []
    for g in range(groups):
        o_ref[g] = encode(sent[g * rows : (g + 1) * rows, :])
        out.append(pltpu.make_async_copy(o_ref.at[g], o_hbm.at[g], o_sem.at[g]))
        out[g].start()
    for copy in out:
        copy.wait()


def same_plane(n):
    i = lax.broadcasted_iota(jnp.int32, (n, n), 0)
    j = lax.broadcasted_iota(jnp.int32, (n, n), 1)
    return lax.rem(i, HP) == lax.rem(j, HP)


def channel_of(lanes):
    i = lax.broadcasted_iota(jnp.int32, (HALF, lanes), 0)
    j = lax.broadcasted_iota(jnp.int32, (HALF, lanes), 1)
    return jnp.where(lax.div(i, HP) == j, 1.0, 0.0).astype(BF)


def half(x, h):
    return x.reshape(C, PL // HP, HP, x.shape[1])[:, h].reshape(HALF, x.shape[1])


def cell_mix_kernel(parts, f_hbm, mix_ref, o_hbm, f_ref, o_ref, sem, o_sem):
    width = f_ref.shape[1] // parts
    copies = chunk_copies([(f_hbm, f_ref)], parts, sem)
    start_chunk(copies, 0)
    e = channel_of(C)
    u = dot(e, mix_ref[...], 1, 1).astype(BF)
    m = jnp.where(same_plane(HALF), dot(u, e, 1, 1), 0.0).astype(BF)
    out = []
    for j in range(parts):
        at = slice(j * width, (j + 1) * width)
        copies[j][0].wait()
        start_chunk(copies, j + 1)
        f = f_ref[:, at]
        for h in range(PL // HP):
            o_ref[:, h, :, at] = dot(m, half(f, h), 1, 0).reshape(C, HP, width)
        out.append(pltpu.make_async_copy(o_ref.at[:, :, :, at], o_hbm.at[:, :, :, at], o_sem.at[j]))
        out[j].start()
    for copy in out:
        copy.wait()


def mix_kernel(groups, rows, r_ref, w_ref, spread_ref, wsel_ref, collect_ref, v_ref, s_ref, wa_ref, wb_ref, vals_ref):
    total = decode(r_ref[0])
    for g in range(1, groups):
        total = total + decode(r_ref[g])
    total = total * (1.0 / (SCALE * math.sqrt(NX * NY)))
    hi, lo = split(total)
    both = jnp.concatenate([hi.astype(F32), lo.astype(F32)], 0).astype(BF)
    s_ref[0, 0:CP, :] = dot(both, spread_ref[:, 0:128], 0, 0)
    s_ref[1, 0:CP, :] = dot(both, spread_ref[:, 128:256], 0, 0)
    s_ref[:, CP:, :] = jnp.zeros((2, CR * PL - CP, 128), F32)
    w = w_ref[...]
    wa_ref[...] = dot(w[:, : C * C], wsel_ref[...], 0, 0)
    wb_ref[...] = dot(w[:, C * C :], wsel_ref[...], 0, 0)

    def some(block, _):
        base = block * 4
        acc = [None] * 4
        for c in range(C):
            s = s_ref[0, c * PL : (c + 1) * PL, :]
            t = s_ref[1, c * PL : (c + 1) * PL, :]
            for k in range(4):
                row = c * C + base + k
                term = s * wa_ref[pl.ds(row, 1), :] + t * wb_ref[pl.ds(row, 1), :]
                acc[k] = term if acc[k] is None else acc[k] + term
        for k in range(4):
            vals_ref[pl.ds(pl.multiple_of((base + k) * PL, PL), PL), :] = acc[k]
        return 0

    lax.fori_loop(0, C // 4, some, 0)
    vals = vals_ref[...] * (1.0 / (SCALE * math.sqrt(MODES)))
    hi, lo = split(vals)
    v_ref[...] = dot(collect_ref[...], jnp.concatenate([hi, lo], 1), 1, 1).astype(BF)


def gelu_both(h):
    k = math.sqrt(2.0 / math.pi)
    h2 = h * h
    t = jnp.tanh(h * (k + (k * 0.044715) * h2))
    half = 0.5 + 0.5 * t
    slope = half + (h * (half * (1.0 - t))) * (k + (3.0 * 0.044715 * k) * h2)
    return h * half, slope


def main_kernel(
    groups, rows, parts, gid_ref, t_hbm, mixed_hbm, cot_hbm, f_hbm, v_ref, out_hbm, o_ref,
    t_ref, mixed_ref, cot_ref, f_ref, out_ref, a_ref, acc_ref, product_ref, t_sem, sem, out_sem,
):
    gid = gid_ref[0]
    width = f_ref.shape[1] // parts
    table_copy = pltpu.make_async_copy(t_hbm.at[gid], t_ref, t_sem.at[0])
    table_copy.start()
    copies = chunk_copies([(mixed_hbm, mixed_ref), (cot_hbm, cot_ref), (f_hbm, f_ref)], parts, sem)
    for j in range(parts):
        start_chunk(copies, j)
    a_ref[...] = jnp.transpose(v_ref[...].astype(F32)).astype(BF)
    table_copy.wait()
    out = []
    for j in range(parts):
        at = slice(j * width, (j + 1) * width)
        t = t_ref[:, at]
        pre = dot(a_ref[...], t, 1, 0)
        for copy in copies[j]:
            copy.wait()
        pre = pre + mixed_ref[:, :, :, at].reshape(CP, width)
        value, slope = gelu_both(pre)
        out_ref[:, at] = value.astype(BF)
        out.append(pltpu.make_async_copy(out_ref.at[:, at], out_hbm.at[:, at], out_sem.at[j]))
        out[j].start()
        back = (cot_ref[:, at].astype(F32) * slope).astype(BF)
        part = dot(t, back, 1, 1)
        f = f_ref[:, at]
        product = dot(half(f, 0), half(back, 0), 1, 1)
        for h in range(1, PL // HP):
            product = product + dot(half(f, h), half(back, h), 1, 1)
        if j == 0:
            acc_ref[...] = part
            product_ref[...] = product
        else:
            acc_ref[...] += part
            product_ref[...] += product
    spectrum = acc_ref[...]
    product = product_ref[...]

    kept = jnp.where(same_plane(HALF), product, 0.0)
    kept = jnp.sum(kept.reshape(C, HP, HALF), axis=1)
    kept = jnp.concatenate([kept, jnp.zeros((CR - C, HALF), F32)], 0)
    hi, lo = split(kept)
    e = channel_of(128)
    y = dot(hi, e, 1, 0) + dot(lo, e, 1, 0)
    yh = y.astype(BF).astype(F32)
    y = yh + pltpu.roll(y - yh, 64, 1)
    extra = jnp.concatenate([y[0:8], y[8:16], y[16:24], jnp.zeros((8, CP - 384), F32)], 1)
    for g in range(groups):
        v = spectrum[g * rows : (g + 1) * rows, :]
        coded = (v * jnp.abs(v)) * (v * v)
        o_ref[g] = jnp.concatenate([coded, extra], 0).astype(BF)
    for copy in out:
        copy.wait()


def grad_kernel(groups, rows, r_ref, s_ref, spread_ref, fold_ref, o_ref, g_ref, p_ref):
    total = None
    extra = None
    for g in range(groups):
        block = r_ref[g].astype(F32)
        y = block[0:rows]
        z = lax.rsqrt(jnp.maximum(jnp.abs(y), 1e-36))
        y = ((y * z) * z) * lax.rsqrt(z)
        total = y if total is None else total + y
        x = block[rows : rows + 8]
        extra = x if extra is None else extra + x
    total = total * (1.0 / (SCALE * math.sqrt(MODES)))
    hi, lo = split(total)
    both = jnp.concatenate([hi.astype(F32), lo.astype(F32)], 0).astype(BF)
    g_ref[...] = dot(both, spread_ref[:, 0:128], 0, 0)

    def some(block, _):
        base = block * 4
        one = [jnp.zeros((CR, 128), F32)] * 4
        two = [jnp.zeros((CR, 128), F32)] * 4
        for p in range(PL):
            s = s_ref[0, pl.ds(p, CR, stride=PL), :]
            t = s_ref[1, pl.ds(p, CR, stride=PL), :]
            for k in range(4):
                g = g_ref[pl.ds((base + k) * PL + p, 1), :]
                one[k] = one[k] + s * g
                two[k] = two[k] + t * g
        for k in range(4):
            at = pl.multiple_of((base + k) * CR, CR)
            p_ref[pl.ds(at, CR), 0:128] = one[k]
            p_ref[pl.ds(at, CR), 128:256] = two[k]
        return 0

    lax.fori_loop(0, C // 4, some, 0)
    hi, lo = split(p_ref[...])
    grads = dot(fold_ref[...], jnp.concatenate([hi, lo], 1), 1, 1)
    grads = jnp.concatenate([grads, jnp.zeros((rows, 512 - C * CR), F32)], 1)
    extra = extra[:, 0:512]
    extra = extra + pltpu.roll(extra, 512 - 64, 1)
    all_rows = jnp.concatenate([grads, extra], 0)
    o_ref[...] = (all_rows * jnp.abs(all_rows)) * (all_rows * all_rows)


def sum_over_dp(coded, samples):
    if samples & (samples - 1):
        parts = lax.all_gather(coded, "dp", axis=0)
        return jnp.sum(decode(parts), axis=0)
    step = 1
    while True:
        other = lax.ppermute(coded, "dp", [(i, i ^ step) for i in range(samples)])
        total = decode(coded) + decode(other)
        step *= 2
        if step >= samples:
            return total
        coded = encode(total)


def compiler_params(mib):
    return pltpu.CompilerParams(vmem_limit_bytes=mib * 2**20)


def local(tables, consts, fields, cotangent, mix_weight, spectral_weight):
    spread, wsel, collect, fold = consts
    cells = fields.shape[3]
    groups = lax.axis_size("gx") * lax.axis_size("gy")
    samples = lax.axis_size("dp")
    per = MODES // groups
    rows = round_up(2 * per, 8)
    flat = fields.reshape(CP, cells)
    cot = cotangent.reshape(CP, cells)
    gid = (lax.axis_index("gx") * lax.axis_size("gy") + lax.axis_index("gy")).astype(jnp.int32).reshape(1)
    parts = max(1, cells // 512)
    halves = max(1, cells // 1024)
    high = groups * rows
    vmem = pl.BlockSpec(memory_space=pltpu.VMEM)
    smem = pl.BlockSpec(memory_space=pltpu.SMEM)

    hbm = pl.BlockSpec(memory_space=pltpu.HBM)
    mixed_shape = (C, PL // HP, HP, cells)

    sent = pl.pallas_call(
        functools.partial(first_kernel, groups, rows, halves),
        in_specs=[smem, hbm, hbm],
        out_specs=hbm,
        out_shape=jax.ShapeDtypeStruct((groups, rows, CP), BF),
        scratch_shapes=[
            pltpu.VMEM((CP, cells), BF),
            pltpu.VMEM((high, cells), BF),
            pltpu.VMEM((high, CP), F32),
            pltpu.VMEM((groups, rows, CP), BF),
            pltpu.SemaphoreType.DMA((2, halves)),
            pltpu.SemaphoreType.DMA((groups,)),
        ],
        compiler_params=compiler_params(60),
        name="spectrum_parts",
    )(gid, flat, tables)
    got = lax.all_to_all(sent, GROUP, 0, 0, tiled=True)

    mixed = pl.pallas_call(
        functools.partial(cell_mix_kernel, parts),
        in_specs=[hbm, vmem],
        out_specs=hbm,
        out_shape=jax.ShapeDtypeStruct(mixed_shape, F32),
        scratch_shapes=[
            pltpu.VMEM((CP, cells), BF),
            pltpu.VMEM(mixed_shape, F32),
            pltpu.SemaphoreType.DMA((1, parts)),
            pltpu.SemaphoreType.DMA((parts,)),
        ],
        compiler_params=compiler_params(60),
        cost_estimate=pl.CostEstimate(flops=2 * 2 * HALF * HALF * cells, bytes_accessed=8 * 2**20, transcendentals=0),
        name="cell_mixing",
    )(flat, mix_weight)

    weights = spectral_weight.reshape(per, 2 * C * C)
    vals, spec = pl.pallas_call(
        functools.partial(mix_kernel, groups, rows),
        out_shape=(jax.ShapeDtypeStruct((rows, CP), BF), jax.ShapeDtypeStruct((2, CR * PL, 128), F32)),
        scratch_shapes=[pltpu.VMEM((C * C, 128), F32), pltpu.VMEM((C * C, 128), F32), pltpu.VMEM((CP, 128), F32)],
        compiler_params=compiler_params(8),
        name="mode_mixing",
    )(got, weights, spread, wsel, collect)
    all_vals = lax.all_gather(vals, GROUP, axis=0, tiled=True)

    output, sent = pl.pallas_call(
        functools.partial(main_kernel, groups, rows, halves),
        in_specs=[smem, hbm, hbm, hbm, hbm, vmem],
        out_specs=(hbm, vmem),
        out_shape=(
            jax.ShapeDtypeStruct((CP, cells), BF),
            jax.ShapeDtypeStruct((groups, rows + 8, CP), BF),
        ),
        scratch_shapes=[
            pltpu.VMEM((high, cells), BF),
            pltpu.VMEM(mixed_shape, F32),
            pltpu.VMEM((CP, cells), BF),
            pltpu.VMEM((CP, cells), BF),
            pltpu.VMEM((CP, cells), BF),
            pltpu.VMEM((CP, high), BF),
            pltpu.VMEM((high, CP), F32),
            pltpu.VMEM((HALF, HALF), F32),
            pltpu.SemaphoreType.DMA((1,)),
            pltpu.SemaphoreType.DMA((3, halves)),
            pltpu.SemaphoreType.DMA((halves,)),
        ],
        compiler_params=compiler_params(48),
        name="cells",
    )(gid, tables, mixed, cot, flat, all_vals)
    got = lax.all_to_all(sent, GROUP, 0, 0, tiled=True)

    coded = pl.pallas_call(
        functools.partial(grad_kernel, groups, rows),
        out_shape=jax.ShapeDtypeStruct((rows + 8, 512), F32),
        scratch_shapes=[pltpu.VMEM((CP, 128), F32), pltpu.VMEM((C * CR, 256), F32)],
        compiler_params=compiler_params(8),
        name="mode_grads",
    )(got, spec, spread, fold)
    total = sum_over_dp(coded.astype(BF), samples)

    grads = total[: 2 * per, : C * CR].reshape(2, per, C, CR)[..., :C]
    spectral_grad = jnp.transpose(grads, (1, 0, 3, 2)) * (1.0 / math.sqrt(samples * PL))
    extra = total[rows:, :384].reshape(8, 3, 128)[:, :, :C]
    mixing = jnp.transpose(extra, (1, 0, 2)).reshape(24, C)[:C]
    mixing_grad = mixing * (1.0 / math.sqrt(samples * PL * NX * NY))
    return (output.reshape(1, C, PL, cells), spectral_grad, mixing_grad)


def solution(mesh):
    groups = mesh.shape["gx"] * mesh.shape["gy"]
    body = functools.partial(local, table(groups), selectors(groups))
    return jax.shard_map(
        body,
        mesh=mesh,
        in_specs=(
            P("dp", None, None, GROUP),
            P("dp", None, None, GROUP),
            P(),
            P(GROUP, None, None, None),
        ),
        out_specs=(P("dp", None, None, GROUP), P(GROUP, None, None, None), P()),
        check_vma=False,
    )
```

```python
import functools
import math

import jax
import jax.numpy as jnp
import ml_dtypes
import numpy as np
from jax import lax
from jax.experimental import pallas as pl
from jax.experimental.pallas import tpu as pltpu
from jax.sharding import PartitionSpec as P

NX = 128
NY = 128
KX = 24
KY = 12
MODES = 288
C = 20
PL = 32
CP = C * PL
HP = 16
HALF = C * HP
CR = 24
SCALE = 1.6656925
GROUP = ("gx", "gy")
BF = jnp.bfloat16
F32 = jnp.float32


def round_up(n, k):
    return -(-n // k) * k


def table(groups):
    per = MODES // groups
    rows = round_up(2 * per, 8)
    index = np.arange(KX)
    waves_x = np.where(index < KX // 2, index, NX - KX + index)
    kx = np.repeat(waves_x, KY)
    ky = np.tile(np.arange(KY), KX)
    x = np.arange(NX * NY) // NY
    y = np.arange(NX * NY) % NY
    turn = (kx[:, None] * x[None] + ky[:, None] * y[None]) % 128
    wheel = 2.0 * np.pi * np.arange(128) / 128
    both = np.stack([(SCALE * np.cos(wheel))[turn], (-SCALE * np.sin(wheel))[turn]], 0)
    both = both.reshape(2, groups, per, -1).transpose(1, 0, 2, 3).reshape(groups, 2 * per, -1)
    full = np.zeros((groups, rows, NX * NY), np.float32)
    full[:, : 2 * per] = both
    full = full.reshape(groups * rows, groups, -1).transpose(1, 0, 2)
    return full.astype(ml_dtypes.bfloat16)


def selectors(groups):
    per = MODES // groups
    rows = round_up(2 * per, 8)
    re, im = np.arange(per), per + np.arange(per)
    spread = np.zeros((rows, 256), np.float32)
    spread[re, re] = 1
    spread[im, im] = 1
    spread[im, 128 + re] = -1
    spread[re, 128 + im] = 1
    weights = np.zeros((per, 128), np.float32)
    weights[re, re] = 1
    weights[re, im] = 1
    collect = np.zeros((rows, 128), np.float32)
    collect[re, re] = 1
    collect[im, im] = 1
    fold = np.zeros((rows, 256), np.float32)
    fold[re, re] = 1
    fold[re, im] = 1
    fold[im, 128 + re] = 1
    fold[im, 128 + im] = 1
    cast = lambda a: a.astype(ml_dtypes.bfloat16)
    return (
        cast(np.concatenate([spread, spread], 0)),
        cast(weights),
        cast(np.concatenate([collect, collect], 1)),
        cast(np.concatenate([fold, fold], 1)),
    )


def dot(a, b, ca, cb):
    return lax.dot_general(a, b, (((ca,), (cb,)), ((), ())), preferred_element_type=F32)


def encode(v):
    return ((v * jnp.abs(v)) * (v * v)).astype(BF)


def decode(y):
    return root(y.astype(F32))


def root(y):
    z = lax.rsqrt(jnp.maximum(jnp.abs(y), 1e-36))
    return ((y * z) * z) * lax.rsqrt(z)


def split(v):
    hi = v.astype(BF)
    return hi, (v - hi.astype(F32)).astype(BF)


def chunk_copies(pairs, parts, sem):
    copies = []
    for j in range(parts):
        copies.append([])
        for k, (source, target) in enumerate(pairs):
            width = target.shape[-1] // parts
            index = (slice(None),) * (len(target.shape) - 1) + (pl.ds(j * width, width),)
            copies[j].append(pltpu.make_async_copy(source.at[index], target.at[index], sem.at[k, j]))
    return copies


def start_chunk(copies, j):
    if j < len(copies):
        for copy in copies[j]:
            copy.start()


def first_kernel(groups, rows, parts, gid_ref, f_hbm, t_hbm, o_hbm, f_ref, t_ref, acc_ref, o_ref, sem, o_sem):
    gid = gid_ref[0]
    width = f_ref.shape[1] // parts
    copies = chunk_copies([(f_hbm, f_ref), (t_hbm.at[gid], t_ref)], parts, sem)
    for j in range(parts):
        start_chunk(copies, j)
    for j in range(parts):
        at = slice(j * width, (j + 1) * width)
        for copy in copies[j]:
            copy.wait()
        part = dot(t_ref[:, at], f_ref[:, at], 1, 1)
        if j == 0:
            acc_ref[...] = part
        elif j < parts - 1:
            acc_ref[...] += part
    sent = acc_ref[...] + part if parts > 1 else part
    out = []
    for g in range(groups):
        o_ref[g] = encode(sent[g * rows : (g + 1) * rows, :])
        out.append(pltpu.make_async_copy(o_ref.at[g], o_hbm.at[g], o_sem.at[g]))
        out[g].start()
    for copy in out:
        copy.wait()


def same_plane(n):
    i = lax.broadcasted_iota(jnp.int32, (n, n), 0)
    j = lax.broadcasted_iota(jnp.int32, (n, n), 1)
    return lax.rem(i, HP) == lax.rem(j, HP)


def channel_of(lanes):
    i = lax.broadcasted_iota(jnp.int32, (HALF, lanes), 0)
    j = lax.broadcasted_iota(jnp.int32, (HALF, lanes), 1)
    return jnp.where(lax.div(i, HP) == j, 1.0, 0.0).astype(BF)


def half(x, h):
    return x.reshape(C, PL // HP, HP, x.shape[1])[:, h].reshape(HALF, x.shape[1])


def cell_mix_kernel(parts, f_hbm, mix_ref, o_hbm, f_ref, o_ref, sem, o_sem):
    width = f_ref.shape[1] // parts
    copies = chunk_copies([(f_hbm, f_ref)], parts, sem)
    start_chunk(copies, 0)
    e = channel_of(C)
    u = dot(e, mix_ref[...], 1, 1).astype(BF)
    m = jnp.where(same_plane(HALF), dot(u, e, 1, 1), 0.0).astype(BF)
    out = []
    for j in range(parts):
        at = slice(j * width, (j + 1) * width)
        copies[j][0].wait()
        start_chunk(copies, j + 1)
        f = f_ref[:, at]
        for h in range(PL // HP):
            o_ref[:, h, :, at] = dot(m, half(f, h), 1, 0).reshape(C, HP, width)
        out.append(pltpu.make_async_copy(o_ref.at[:, :, :, at], o_hbm.at[:, :, :, at], o_sem.at[j]))
        out[j].start()
    for copy in out:
        copy.wait()


def mix_kernel(groups, rows, r_ref, w_ref, spread_ref, wsel_ref, collect_ref, v_ref, s_ref, wa_ref, wb_ref, vals_ref):
    total = decode(r_ref[0])
    for g in range(1, groups):
        total = total + decode(r_ref[g])
    total = total * (1.0 / (SCALE * math.sqrt(NX * NY)))
    hi, lo = split(total)
    both = jnp.concatenate([hi.astype(F32), lo.astype(F32)], 0).astype(BF)
    s_ref[0, 0:CP, :] = dot(both, spread_ref[:, 0:128], 0, 0)
    s_ref[1, 0:CP, :] = dot(both, spread_ref[:, 128:256], 0, 0)
    s_ref[:, CP:, :] = jnp.zeros((2, CR * PL - CP, 128), F32)
    w = w_ref[...]
    wa_ref[...] = dot(w[:, : C * C], wsel_ref[...], 0, 0)
    wb_ref[...] = dot(w[:, C * C :], wsel_ref[...], 0, 0)

    def some(block, _):
        base = block * 4
        acc = [None] * 4
        for c in range(C):
            s = s_ref[0, c * PL : (c + 1) * PL, :]
            t = s_ref[1, c * PL : (c + 1) * PL, :]
            for k in range(4):
                row = c * C + base + k
                term = s * wa_ref[pl.ds(row, 1), :] + t * wb_ref[pl.ds(row, 1), :]
                acc[k] = term if acc[k] is None else acc[k] + term
        for k in range(4):
            vals_ref[pl.ds(pl.multiple_of((base + k) * PL, PL), PL), :] = acc[k]
        return 0

    lax.fori_loop(0, C // 4, some, 0)
    vals = vals_ref[...] * (1.0 / (SCALE * math.sqrt(MODES)))
    hi, lo = split(vals)
    v_ref[...] = dot(collect_ref[...], jnp.concatenate([hi, lo], 1), 1, 1).astype(BF)


def gelu_both(h):
    k = math.sqrt(2.0 / math.pi)
    h2 = h * h
    t = jnp.tanh(h * (k + (k * 0.044715) * h2))
    half = 0.5 + 0.5 * t
    slope = half + (h * (half * (1.0 - t))) * (k + (3.0 * 0.044715 * k) * h2)
    return h * half, slope


def main_kernel(
    groups, rows, parts, gid_ref, t_hbm, mixed_hbm, cot_hbm, f_hbm, v_ref, out_hbm, o_ref,
    t_ref, mixed_ref, cot_ref, f_ref, out_ref, a_ref, acc_ref, product_ref, t_sem, sem, out_sem,
):
    gid = gid_ref[0]
    width = f_ref.shape[1] // parts
    table_copy = pltpu.make_async_copy(t_hbm.at[gid], t_ref, t_sem.at[0])
    table_copy.start()
    copies = chunk_copies([(mixed_hbm, mixed_ref), (cot_hbm, cot_ref), (f_hbm, f_ref)], parts, sem)
    for j in range(parts):
        start_chunk(copies, j)
    a_ref[...] = jnp.transpose(v_ref[...].astype(F32)).astype(BF)
    table_copy.wait()
    out = []
    for j in range(parts):
        at = slice(j * width, (j + 1) * width)
        t = t_ref[:, at]
        pre = dot(a_ref[...], t, 1, 0)
        for copy in copies[j]:
            copy.wait()
        pre = pre + mixed_ref[:, :, :, at].reshape(CP, width)
        value, slope = gelu_both(pre)
        out_ref[:, at] = value.astype(BF)
        out.append(pltpu.make_async_copy(out_ref.at[:, at], out_hbm.at[:, at], out_sem.at[j]))
        out[j].start()
        back = (cot_ref[:, at].astype(F32) * slope).astype(BF)
        part = dot(t, back, 1, 1)
        f = f_ref[:, at]
        product = dot(half(f, 0), half(back, 0), 1, 1)
        for h in range(1, PL // HP):
            product = product + dot(half(f, h), half(back, h), 1, 1)
        if j == 0:
            acc_ref[...] = part
            product_ref[...] = product
        else:
            acc_ref[...] += part
            product_ref[...] += product
    spectrum = acc_ref[...]
    product = product_ref[...]

    kept = jnp.where(same_plane(HALF), product, 0.0)
    kept = jnp.sum(kept.reshape(C, HP, HALF), axis=1)
    kept = jnp.concatenate([kept, jnp.zeros((CR - C, HALF), F32)], 0)
    hi, lo = split(kept)
    e = channel_of(128)
    y = dot(hi, e, 1, 0) + dot(lo, e, 1, 0)
    yh = y.astype(BF).astype(F32)
    y = yh + pltpu.roll(y - yh, 64, 1)
    extra = y[0:8] + pltpu.roll(y[8:16], C, 1) + pltpu.roll(y[16:24], 2 * C, 1)
    for g in range(groups):
        v = spectrum[g * rows : (g + 1) * rows, :]
        coded = (v * jnp.abs(v)) * (v * v)
        tiles = [coded[:, 128 * i : 128 * (i + 1)] for i in range(CP // 128)]
        o_ref[g] = jnp.concatenate(tiles + [extra], 0).astype(BF)
    for copy in out:
        copy.wait()


def payload_rows(rows):
    return round_up(3 * rows + 16, 16)


def grad_kernel(groups, rows, r_ref, s_ref, spread_ref, fold_ref, o_ref, g_ref, p_ref):
    high = rows * CP // 128
    total = None
    extra = None
    for g in range(groups):
        block = r_ref[g].astype(F32)
        y = root(block[0:high])
        total = y if total is None else total + y
        x = block[high : high + 8]
        extra = x if extra is None else extra + x
    total = total * (1.0 / (SCALE * math.sqrt(MODES)))
    total = jnp.concatenate([total[i * rows : (i + 1) * rows] for i in range(CP // 128)], 1)
    hi, lo = split(total)
    both = jnp.concatenate([hi.astype(F32), lo.astype(F32)], 0).astype(BF)
    g_ref[0:CP, :] = dot(both, spread_ref[:, 0:128], 0, 0)
    g_ref[CP:, :] = jnp.zeros((CR * PL - CP, 128), F32)

    def some(block, _):
        base = block * 5
        one = [jnp.zeros((CR, 128), F32)] * 5
        two = [jnp.zeros((CR, 128), F32)] * 5
        for p in range(PL):
            g = g_ref[pl.ds(p, CR, stride=PL), :]
            for k in range(5):
                one[k] = one[k] + s_ref[0, pl.ds((base + k) * PL + p, 1), :] * g
                two[k] = two[k] + s_ref[1, pl.ds((base + k) * PL + p, 1), :] * g
        for k in range(5):
            at = pl.multiple_of((base + k) * CR, CR)
            p_ref[pl.ds(at, CR), 0:128] = one[k]
            p_ref[pl.ds(at, CR), 128:256] = two[k]
        return 0

    lax.fori_loop(0, C // 5, some, 0)
    products = jnp.concatenate([p_ref[c * CR : c * CR + C, :] for c in range(C)], 0)
    hi, lo = split(products)
    grads = dot(fold_ref[...], jnp.concatenate([hi, lo], 1), 1, 1)
    tail = jnp.concatenate([grads[:, 384:], jnp.zeros((rows, 512 - C * C), F32)], 1)
    lane = lax.broadcasted_iota(jnp.int32, (8, 128), 1)
    extra = extra + pltpu.roll(extra, 64, 1)
    extra = jnp.where(lane < 3 * C, extra, 0.0)
    strip = [jnp.zeros((8, 128), F32), pltpu.roll(extra, 64, 1)]
    for i in range(rows // 8):
        piece = tail[8 * i : 8 * i + 8]
        strip[i // 8] = strip[i // 8] + (pltpu.roll(piece, 16 * (i % 8), 1) if i % 8 else piece)
    fill = jnp.zeros((payload_rows(rows) - 3 * rows - 16, 128), F32)
    parts = [grads[:, 128 * i : 128 * (i + 1)] for i in range(3)] + strip
    if fill.shape[0]:
        parts.append(fill)
    o_ref[...] = encode(jnp.concatenate(parts, 0))


def last_kernel(rows, per, samples, own_ref, other_ref, grad_ref, mix_ref):
    total = decode(own_ref[...])
    total = total + decode(other_ref[...])
    lane = lax.broadcasted_iota(jnp.int32, (8, 128), 1)
    strip = [total[3 * rows : 3 * rows + 8], total[3 * rows + 8 : 3 * rows + 16]]
    tail = []
    for i in range(rows // 8):
        piece = pltpu.roll(strip[i // 8], 128 - 16 * (i % 8), 1) if i % 8 else strip[i // 8]
        tail.append(jnp.where(lane < C * C - 384, piece, 0.0))
    grads = jnp.concatenate([total[i * rows : (i + 1) * rows] for i in range(3)] + [jnp.concatenate(tail, 0)], 1)
    grads = jnp.transpose(grads * (1.0 / math.sqrt(samples * PL)))[0 : C * C]
    grad_ref[:, 0, :] = grads[:, 0:per]
    grad_ref[:, 1, :] = grads[:, per : 2 * per]
    mix = strip[1] * (1.0 / math.sqrt(samples * PL * NX * NY))
    mix_ref[0:8, :] = pltpu.roll(mix, 64, 1)[:, 0:C]
    mix_ref[8:16, :] = pltpu.roll(mix, 64 - C, 1)[:, 0:C]
    mix_ref[16:C, :] = pltpu.roll(mix, 64 - 2 * C, 1)[0 : C - 16, 0:C]


def sum_over_dp(coded, samples):
    if samples & (samples - 1) or samples == 1:
        total = jnp.sum(decode(lax.all_gather(coded, "dp", axis=0)), axis=0)
        return encode(total), jnp.zeros_like(coded)
    step = 1
    while True:
        other = lax.ppermute(coded, "dp", [(i, i ^ step) for i in range(samples)])
        step *= 2
        if step >= samples:
            return coded, other
        coded = encode(decode(coded) + decode(other))


def compiler_params(mib):
    return pltpu.CompilerParams(vmem_limit_bytes=mib * 2**20)


def local(tables, consts, fields, cotangent, mix_weight, spectral_weight):
    spread, wsel, collect, fold = consts
    cells = fields.shape[3]
    groups = lax.axis_size("gx") * lax.axis_size("gy")
    samples = lax.axis_size("dp")
    per = MODES // groups
    rows = round_up(2 * per, 8)
    flat = fields.reshape(CP, cells)
    cot = cotangent.reshape(CP, cells)
    gid = (lax.axis_index("gx") * lax.axis_size("gy") + lax.axis_index("gy")).astype(jnp.int32).reshape(1)
    parts = max(1, cells // 512)
    halves = max(1, cells // 1024)
    high = groups * rows
    vmem = pl.BlockSpec(memory_space=pltpu.VMEM)
    smem = pl.BlockSpec(memory_space=pltpu.SMEM)

    hbm = pl.BlockSpec(memory_space=pltpu.HBM)
    mixed_shape = (C, PL // HP, HP, cells)

    sent = pl.pallas_call(
        functools.partial(first_kernel, groups, rows, halves),
        in_specs=[smem, hbm, hbm],
        out_specs=hbm,
        out_shape=jax.ShapeDtypeStruct((groups, rows, CP), BF),
        scratch_shapes=[
            pltpu.VMEM((CP, cells), BF),
            pltpu.VMEM((high, cells), BF),
            pltpu.VMEM((high, CP), F32),
            pltpu.VMEM((groups, rows, CP), BF),
            pltpu.SemaphoreType.DMA((2, halves)),
            pltpu.SemaphoreType.DMA((groups,)),
        ],
        compiler_params=compiler_params(60),
        name="spectrum_parts",
    )(gid, flat, tables)
    got = lax.all_to_all(sent, GROUP, 0, 0, tiled=True)

    mixed = pl.pallas_call(
        functools.partial(cell_mix_kernel, parts),
        in_specs=[hbm, vmem],
        out_specs=hbm,
        out_shape=jax.ShapeDtypeStruct(mixed_shape, F32),
        scratch_shapes=[
            pltpu.VMEM((CP, cells), BF),
            pltpu.VMEM(mixed_shape, F32),
            pltpu.SemaphoreType.DMA((1, parts)),
            pltpu.SemaphoreType.DMA((parts,)),
        ],
        compiler_params=compiler_params(60),
        cost_estimate=pl.CostEstimate(flops=2 * 2 * HALF * HALF * cells, bytes_accessed=8 * 2**20, transcendentals=0),
        name="cell_mixing",
    )(flat, mix_weight)

    weights = spectral_weight.reshape(per, 2 * C * C)
    vals, spec = pl.pallas_call(
        functools.partial(mix_kernel, groups, rows),
        out_shape=(jax.ShapeDtypeStruct((rows, CP), BF), jax.ShapeDtypeStruct((2, CR * PL, 128), F32)),
        scratch_shapes=[pltpu.VMEM((C * C, 128), F32), pltpu.VMEM((C * C, 128), F32), pltpu.VMEM((CP, 128), F32)],
        compiler_params=compiler_params(8),
        name="mode_mixing",
    )(got, weights, spread, wsel, collect)
    all_vals = lax.all_gather(vals, GROUP, axis=0, tiled=True)

    output, sent = pl.pallas_call(
        functools.partial(main_kernel, groups, rows, halves),
        in_specs=[smem, hbm, hbm, hbm, hbm, vmem],
        out_specs=(hbm, vmem),
        out_shape=(
            jax.ShapeDtypeStruct((CP, cells), BF),
            jax.ShapeDtypeStruct((groups, rows * CP // 128 + 8, 128), BF),
        ),
        scratch_shapes=[
            pltpu.VMEM((high, cells), BF),
            pltpu.VMEM(mixed_shape, F32),
            pltpu.VMEM((CP, cells), BF),
            pltpu.VMEM((CP, cells), BF),
            pltpu.VMEM((CP, cells), BF),
            pltpu.VMEM((CP, high), BF),
            pltpu.VMEM((high, CP), F32),
            pltpu.VMEM((HALF, HALF), F32),
            pltpu.SemaphoreType.DMA((1,)),
            pltpu.SemaphoreType.DMA((3, halves)),
            pltpu.SemaphoreType.DMA((halves,)),
        ],
        compiler_params=compiler_params(48),
        name="cells",
    )(gid, tables, mixed, cot, flat, all_vals)
    got = lax.all_to_all(sent, GROUP, 0, 0, tiled=True)

    coded = pl.pallas_call(
        functools.partial(grad_kernel, groups, rows),
        out_shape=jax.ShapeDtypeStruct((payload_rows(rows), 128), BF),
        scratch_shapes=[pltpu.VMEM((CR * PL, 128), F32), pltpu.VMEM((C * CR, 256), F32)],
        compiler_params=compiler_params(8),
        name="mode_grads",
    )(got, spec, spread, fold)
    own, other = sum_over_dp(coded, samples)
    grads, mixing_grad = pl.pallas_call(
        functools.partial(last_kernel, rows, per, samples),
        out_shape=(jax.ShapeDtypeStruct((C * C, 2, per), F32), jax.ShapeDtypeStruct((C, C), F32)),
        compiler_params=compiler_params(8),
        name="gradients_out",
    )(own, other)
    spectral_grad = jnp.transpose(grads.reshape(C, C, 2, per), (3, 2, 0, 1))
    return (output.reshape(1, C, PL, cells), spectral_grad, mixing_grad)


def solution(mesh):
    groups = mesh.shape["gx"] * mesh.shape["gy"]
    body = functools.partial(local, table(groups), selectors(groups))
    return jax.shard_map(
        body,
        mesh=mesh,
        in_specs=(
            P("dp", None, None, GROUP),
            P("dp", None, None, GROUP),
            P(),
            P(GROUP, None, None, None),
        ),
        out_specs=(P("dp", None, None, GROUP), P(GROUP, None, None, None), P()),
        check_vma=False,
    )
```

```python
import functools
import math

import jax
import jax.numpy as jnp
import ml_dtypes
import numpy as np
from jax import lax
from jax.experimental import pallas as pl
from jax.experimental.pallas import tpu as pltpu
from jax.sharding import PartitionSpec as P

NX = 128
NY = 128
KX = 24
KY = 12
MODES = 288
C = 20
PL = 32
CP = C * PL
HP = 16
HALF = C * HP
CR = 24
SCALE = 1.6656925
GROUP = ("gx", "gy")
BF = jnp.bfloat16
F32 = jnp.float32


def round_up(n, k):
    return -(-n // k) * k


def table(groups):
    per = MODES // groups
    rows = round_up(2 * per, 8)
    index = np.arange(KX)
    waves_x = np.where(index < KX // 2, index, NX - KX + index)
    kx = np.repeat(waves_x, KY)
    ky = np.tile(np.arange(KY), KX)
    x = np.arange(NX * NY) // NY
    y = np.arange(NX * NY) % NY
    turn = (kx[:, None] * x[None] + ky[:, None] * y[None]) % 128
    wheel = 2.0 * np.pi * np.arange(128) / 128
    both = np.stack([(SCALE * np.cos(wheel))[turn], (-SCALE * np.sin(wheel))[turn]], 0)
    both = both.reshape(2, groups, per, -1).transpose(1, 0, 2, 3).reshape(groups, 2 * per, -1)
    full = np.zeros((groups, rows, NX * NY), np.float32)
    full[:, : 2 * per] = both
    full = full.reshape(groups * rows, groups, -1).transpose(1, 0, 2)
    return full.astype(ml_dtypes.bfloat16)


def selectors(groups):
    per = MODES // groups
    rows = round_up(2 * per, 8)
    re, im = np.arange(per), per + np.arange(per)
    spread = np.zeros((rows, 256), np.float32)
    spread[re, re] = 1
    spread[im, im] = 1
    spread[im, 128 + re] = -1
    spread[re, 128 + im] = 1
    weights = np.zeros((per, 128), np.float32)
    weights[re, re] = 1
    weights[re, im] = 1
    collect = np.zeros((rows, 128), np.float32)
    collect[re, re] = 1
    collect[im, im] = 1
    fold = np.zeros((rows, 256), np.float32)
    fold[re, re] = 1
    fold[re, im] = 1
    fold[im, 128 + re] = 1
    fold[im, 128 + im] = 1
    cast = lambda a: a.astype(ml_dtypes.bfloat16)
    return (
        cast(np.concatenate([spread, spread], 0)),
        cast(weights),
        cast(np.concatenate([collect, collect], 1)),
        cast(np.concatenate([fold, fold], 1)),
    )


def dot(a, b, ca, cb):
    return lax.dot_general(a, b, (((ca,), (cb,)), ((), ())), preferred_element_type=F32)


def encode(v):
    return ((v * jnp.abs(v)) * (v * v)).astype(BF)


def decode(y):
    return root(y.astype(F32))


def root(y):
    z = lax.rsqrt(jnp.maximum(jnp.abs(y), 1e-36))
    return ((y * z) * z) * lax.rsqrt(z)


def split(v):
    hi = v.astype(BF)
    return hi, (v - hi.astype(F32)).astype(BF)


def chunk_copies(pairs, parts, sem):
    copies = []
    for j in range(parts):
        copies.append([])
        for k, (source, target) in enumerate(pairs):
            width = target.shape[-1] // parts
            index = (slice(None),) * (len(target.shape) - 1) + (pl.ds(j * width, width),)
            copies[j].append(pltpu.make_async_copy(source.at[index], target.at[index], sem.at[k, j]))
    return copies


def start_chunk(copies, j):
    if j < len(copies):
        for copy in copies[j]:
            copy.start()


def first_kernel(groups, rows, parts, gid_ref, f_hbm, t_hbm, o_ref, f_ref, t_ref, acc_ref, sem):
    gid = gid_ref[0]
    width = f_ref.shape[1] // parts
    copies = chunk_copies([(f_hbm, f_ref), (t_hbm.at[gid], t_ref)], parts, sem)
    for j in range(parts):
        start_chunk(copies, j)
    for j in range(parts):
        at = slice(j * width, (j + 1) * width)
        for copy in copies[j]:
            copy.wait()
        part = dot(t_ref[:, at], f_ref[:, at], 1, 1)
        if j == 0:
            acc_ref[...] = part
        elif j < parts - 1:
            acc_ref[...] += part
    sent = acc_ref[...] + part if parts > 1 else part
    for g in range(groups):
        o_ref[g] = encode(sent[g * rows : (g + 1) * rows, :])


def same_plane(n):
    i = lax.broadcasted_iota(jnp.int32, (n, n), 0)
    j = lax.broadcasted_iota(jnp.int32, (n, n), 1)
    return lax.rem(i, HP) == lax.rem(j, HP)


def channel_of(lanes):
    i = lax.broadcasted_iota(jnp.int32, (HALF, lanes), 0)
    j = lax.broadcasted_iota(jnp.int32, (HALF, lanes), 1)
    return jnp.where(lax.div(i, HP) == j, 1.0, 0.0).astype(BF)


def half(x, h):
    return x.reshape(C, PL // HP, HP, x.shape[1])[:, h].reshape(HALF, x.shape[1])


def mix_kernel(
    groups, rows, cot_hbm, r_ref, w_ref, spread_ref, wsel_ref, collect_ref, v_ref, s_ref, cot_ref,
    wa_ref, wb_ref, vals_ref, sem,
):
    cot_copy = pltpu.make_async_copy(cot_hbm, cot_ref, sem.at[0])
    cot_copy.start()
    total = decode(r_ref[0])
    for g in range(1, groups):
        total = total + decode(r_ref[g])
    total = total * (1.0 / (SCALE * math.sqrt(NX * NY)))
    hi, lo = split(total)
    both = jnp.concatenate([hi.astype(F32), lo.astype(F32)], 0).astype(BF)
    s_ref[0, 0:CP, :] = dot(both, spread_ref[:, 0:128], 0, 0)
    s_ref[1, 0:CP, :] = dot(both, spread_ref[:, 128:256], 0, 0)
    s_ref[:, CP:, :] = jnp.zeros((2, CR * PL - CP, 128), F32)
    w = w_ref[...].astype(F32)
    wa_ref[...] = dot(w[:, 0, :].astype(BF), wsel_ref[...], 1, 0)
    wb_ref[...] = dot(w[:, 1, :].astype(BF), wsel_ref[...], 1, 0)

    def some(block, _):
        base = block * 4
        acc = [None] * 4
        for c in range(C):
            s = s_ref[0, c * PL : (c + 1) * PL, :]
            t = s_ref[1, c * PL : (c + 1) * PL, :]
            for k in range(4):
                row = c * C + base + k
                term = s * wa_ref[pl.ds(row, 1), :] + t * wb_ref[pl.ds(row, 1), :]
                acc[k] = term if acc[k] is None else acc[k] + term
        for k in range(4):
            vals_ref[pl.ds(pl.multiple_of((base + k) * PL, PL), PL), :] = acc[k]
        return 0

    lax.fori_loop(0, C // 4, some, 0)
    vals = vals_ref[...] * (1.0 / (SCALE * math.sqrt(MODES)))
    hi, lo = split(vals)
    v_ref[...] = dot(collect_ref[...], jnp.concatenate([hi, lo], 1), 1, 1).astype(BF)
    cot_copy.wait()


def gelu_both(h):
    k = math.sqrt(2.0 / math.pi)
    h2 = h * h
    t = jnp.tanh(h * (k + (k * 0.044715) * h2))
    half = 0.5 + 0.5 * t
    slope = half + (h * (half * (1.0 - t))) * (k + (3.0 * 0.044715 * k) * h2)
    return h * half, slope


def main_kernel(
    groups, rows, parts, t_ref, f_ref, cot_ref, v_ref, mix_ref, out_hbm, o_ref,
    out_ref, a_ref, acc_ref, product_ref, out_sem,
):
    width = f_ref.shape[1] // parts
    vals = jnp.transpose(v_ref[...].astype(F32))
    e = channel_of(C)
    m = jnp.where(same_plane(HALF), dot(dot(e, mix_ref[...], 1, 1).astype(BF), e, 1, 1), 0.0)
    for h in range(PL // HP):
        a_ref[h] = jnp.concatenate([half(vals, h), m], 1).astype(BF)
    out = []
    for j in range(parts):
        at = slice(j * width, (j + 1) * width)
        t = t_ref[:, at]
        f = f_ref[:, at]
        pre = [dot(a_ref[h], jnp.concatenate([t, half(f, h)], 0), 1, 0) for h in range(PL // HP)]
        pre = jnp.stack([x.reshape(C, HP, width) for x in pre], 1).reshape(CP, width)
        value, slope = gelu_both(pre)
        out_ref[:, at] = value.astype(BF)
        out.append(pltpu.make_async_copy(out_ref.at[:, at], out_hbm.at[:, at], out_sem.at[j]))
        out[j].start()
        back = (cot_ref[:, at].astype(F32) * slope).astype(BF)
        part = dot(t, back, 1, 1)
        product = dot(half(f, 0), half(back, 0), 1, 1)
        for h in range(1, PL // HP):
            product = product + dot(half(f, h), half(back, h), 1, 1)
        if j == 0:
            acc_ref[...] = part
            product_ref[...] = product
        else:
            acc_ref[...] += part
            product_ref[...] += product
    spectrum = acc_ref[...]
    product = product_ref[...]

    kept = jnp.where(same_plane(HALF), product, 0.0)
    kept = jnp.sum(kept.reshape(C, HP, HALF), axis=1)
    kept = jnp.concatenate([kept, jnp.zeros((CR - C, HALF), F32)], 0)
    hi, lo = split(kept)
    e = channel_of(128)
    y = dot(hi, e, 1, 0) + dot(lo, e, 1, 0)
    yh = y.astype(BF).astype(F32)
    y = yh + pltpu.roll(y - yh, 64, 1)
    extra = y[0:8] + pltpu.roll(y[8:16], C, 1) + pltpu.roll(y[16:24], 2 * C, 1)
    for g in range(groups):
        v = spectrum[g * rows : (g + 1) * rows, :]
        coded = (v * jnp.abs(v)) * (v * v)
        tiles = [coded[:, 128 * i : 128 * (i + 1)] for i in range(CP // 128)]
        o_ref[g] = jnp.concatenate(tiles + [extra], 0).astype(BF)
    for copy in out:
        copy.wait()


def payload_rows(rows):
    return round_up(3 * rows + 16, 16)


def grad_kernel(groups, rows, r_ref, s_ref, spread_ref, fold_ref, o_ref, g_ref, p_ref):
    high = rows * CP // 128
    total = None
    extra = None
    for g in range(groups):
        block = r_ref[g].astype(F32)
        y = root(block[0:high])
        total = y if total is None else total + y
        x = block[high : high + 8]
        extra = x if extra is None else extra + x
    total = total * (1.0 / (SCALE * math.sqrt(MODES)))
    total = jnp.concatenate([total[i * rows : (i + 1) * rows] for i in range(CP // 128)], 1)
    hi, lo = split(total)
    both = jnp.concatenate([hi.astype(F32), lo.astype(F32)], 0).astype(BF)
    g_ref[0:CP, :] = dot(both, spread_ref[:, 0:128], 0, 0)
    g_ref[CP:, :] = jnp.zeros((CR * PL - CP, 128), F32)

    def some(block, _):
        base = block * 5
        one = [jnp.zeros((CR, 128), F32)] * 5
        two = [jnp.zeros((CR, 128), F32)] * 5
        for p in range(PL):
            g = g_ref[pl.ds(p, CR, stride=PL), :]
            for k in range(5):
                one[k] = one[k] + s_ref[0, pl.ds((base + k) * PL + p, 1), :] * g
                two[k] = two[k] + s_ref[1, pl.ds((base + k) * PL + p, 1), :] * g
        for k in range(5):
            at = pl.multiple_of((base + k) * CR, CR)
            p_ref[pl.ds(at, CR), 0:128] = one[k]
            p_ref[pl.ds(at, CR), 128:256] = two[k]
        return 0

    lax.fori_loop(0, C // 5, some, 0)
    products = jnp.concatenate([p_ref[c * CR : c * CR + C, :] for c in range(C)], 0)
    hi, lo = split(products)
    grads = dot(fold_ref[...], jnp.concatenate([hi, lo], 1), 1, 1)
    tail = jnp.concatenate([grads[:, 384:], jnp.zeros((rows, 512 - C * C), F32)], 1)
    lane = lax.broadcasted_iota(jnp.int32, (8, 128), 1)
    extra = extra + pltpu.roll(extra, 64, 1)
    extra = jnp.where(lane < 3 * C, extra, 0.0)
    strip = [jnp.zeros((8, 128), F32), pltpu.roll(extra, 64, 1)]
    for i in range(rows // 8):
        piece = tail[8 * i : 8 * i + 8]
        strip[i // 8] = strip[i // 8] + (pltpu.roll(piece, 16 * (i % 8), 1) if i % 8 else piece)
    fill = jnp.zeros((payload_rows(rows) - 3 * rows - 16, 128), F32)
    parts = [grads[:, 128 * i : 128 * (i + 1)] for i in range(3)] + strip
    if fill.shape[0]:
        parts.append(fill)
    o_ref[...] = encode(jnp.concatenate(parts, 0))


def last_kernel(rows, per, samples, own_ref, other_ref, grad_ref, mix_ref):
    total = decode(own_ref[...])
    total = total + decode(other_ref[...])
    lane = lax.broadcasted_iota(jnp.int32, (8, 128), 1)
    strip = [total[3 * rows : 3 * rows + 8], total[3 * rows + 8 : 3 * rows + 16]]
    tail = []
    for i in range(rows // 8):
        piece = pltpu.roll(strip[i // 8], 128 - 16 * (i % 8), 1) if i % 8 else strip[i // 8]
        tail.append(jnp.where(lane < C * C - 384, piece, 0.0))
    grads = jnp.concatenate([total[i * rows : (i + 1) * rows] for i in range(3)] + [jnp.concatenate(tail, 0)], 1)
    grads = jnp.transpose(grads * (1.0 / math.sqrt(samples * PL)))[0 : C * C]
    grad_ref[:, 0, :] = grads[:, 0:per]
    grad_ref[:, 1, :] = grads[:, per : 2 * per]
    mix = strip[1] * (1.0 / math.sqrt(samples * PL * NX * NY))
    mix_ref[0:8, :] = pltpu.roll(mix, 64, 1)[:, 0:C]
    mix_ref[8:16, :] = pltpu.roll(mix, 64 - C, 1)[:, 0:C]
    mix_ref[16:C, :] = pltpu.roll(mix, 64 - 2 * C, 1)[0 : C - 16, 0:C]


def sum_over_dp(coded, samples):
    if samples & (samples - 1) or samples == 1:
        total = jnp.sum(decode(lax.all_gather(coded, "dp", axis=0)), axis=0)
        return encode(total), jnp.zeros_like(coded)
    step = 1
    while True:
        other = lax.ppermute(coded, "dp", [(i, i ^ step) for i in range(samples)])
        step *= 2
        if step >= samples:
            return coded, other
        coded = encode(decode(coded) + decode(other))


def compiler_params(mib):
    return pltpu.CompilerParams(vmem_limit_bytes=mib * 2**20)


def local(tables, consts, fields, cotangent, mix_weight, spectral_weight):
    spread, wsel, collect, fold = consts
    cells = fields.shape[3]
    groups = lax.axis_size("gx") * lax.axis_size("gy")
    samples = lax.axis_size("dp")
    per = MODES // groups
    rows = round_up(2 * per, 8)
    flat = fields.reshape(CP, cells)
    cot = cotangent.reshape(CP, cells)
    gid = (lax.axis_index("gx") * lax.axis_size("gy") + lax.axis_index("gy")).astype(jnp.int32).reshape(1)
    halves = max(1, cells // 1024)
    high = groups * rows
    vmem = pl.BlockSpec(memory_space=pltpu.VMEM)
    smem = pl.BlockSpec(memory_space=pltpu.SMEM)

    hbm = pl.BlockSpec(memory_space=pltpu.HBM)

    sent, flat_in, table_in = pl.pallas_call(
        functools.partial(first_kernel, groups, rows, halves),
        in_specs=[smem, hbm, hbm],
        out_specs=(vmem, vmem, vmem),
        out_shape=(
            jax.ShapeDtypeStruct((groups, rows, CP), BF),
            jax.ShapeDtypeStruct((CP, cells), BF),
            jax.ShapeDtypeStruct((high, cells), BF),
        ),
        scratch_shapes=[
            pltpu.VMEM((high, CP), F32),
            pltpu.SemaphoreType.DMA((2, halves)),
        ],
        compiler_params=compiler_params(50),
        name="spectrum_parts",
    )(gid, flat, tables)
    got = lax.all_to_all(sent, GROUP, 0, 0, tiled=True)

    weights = jnp.transpose(spectral_weight, (2, 3, 1, 0)).reshape(C * C, 2, per)
    vals, spec, cot_in = pl.pallas_call(
        functools.partial(mix_kernel, groups, rows),
        in_specs=[hbm] + [vmem] * 5,
        out_specs=[vmem] * 3,
        out_shape=[
            jax.ShapeDtypeStruct((rows, CP), BF),
            jax.ShapeDtypeStruct((2, CR * PL, 128), F32),
            jax.ShapeDtypeStruct((CP, cells), BF),
        ],
        scratch_shapes=[
            pltpu.VMEM((C * C, 128), F32),
            pltpu.VMEM((C * C, 128), F32),
            pltpu.VMEM((CP, 128), F32),
            pltpu.SemaphoreType.DMA((1,)),
        ],
        compiler_params=compiler_params(48),
        name="mode_mixing",
    )(cot, got, weights, spread, wsel, collect)
    all_vals = lax.all_gather(vals, GROUP, axis=0, tiled=True)

    output, sent = pl.pallas_call(
        functools.partial(main_kernel, groups, rows, 1),
        in_specs=[vmem] * 5,
        out_specs=(hbm, vmem),
        out_shape=(
            jax.ShapeDtypeStruct((CP, cells), BF),
            jax.ShapeDtypeStruct((groups, rows * CP // 128 + 8, 128), BF),
        ),
        scratch_shapes=[
            pltpu.VMEM((CP, cells), BF),
            pltpu.VMEM((PL // HP, HALF, high + HALF), BF),
            pltpu.VMEM((high, CP), F32),
            pltpu.VMEM((HALF, HALF), F32),
            pltpu.SemaphoreType.DMA((1,)),
        ],
        compiler_params=compiler_params(40),
        name="cells",
    )(table_in, flat_in, cot_in, all_vals, mix_weight)
    got = lax.all_to_all(sent, GROUP, 0, 0, tiled=True)

    coded = pl.pallas_call(
        functools.partial(grad_kernel, groups, rows),
        out_shape=jax.ShapeDtypeStruct((payload_rows(rows), 128), BF),
        scratch_shapes=[pltpu.VMEM((CR * PL, 128), F32), pltpu.VMEM((C * CR, 256), F32)],
        compiler_params=compiler_params(8),
        name="mode_grads",
    )(got, spec, spread, fold)
    own, other = sum_over_dp(coded, samples)
    grads, mixing_grad = pl.pallas_call(
        functools.partial(last_kernel, rows, per, samples),
        out_shape=(jax.ShapeDtypeStruct((C * C, 2, per), F32), jax.ShapeDtypeStruct((C, C), F32)),
        compiler_params=compiler_params(8),
        name="gradients_out",
    )(own, other)
    spectral_grad = jnp.transpose(grads.reshape(C, C, 2, per), (3, 2, 0, 1))
    return (output.reshape(1, C, PL, cells), spectral_grad, mixing_grad)


def solution(mesh):
    groups = mesh.shape["gx"] * mesh.shape["gy"]
    body = functools.partial(local, table(groups), selectors(groups))
    return jax.shard_map(
        body,
        mesh=mesh,
        in_specs=(
            P("dp", None, None, GROUP),
            P("dp", None, None, GROUP),
            P(),
            P(GROUP, None, None, None),
        ),
        out_specs=(P("dp", None, None, GROUP), P(GROUP, None, None, None), P()),
        check_vma=False,
    )
```

```python
import functools
import math

import jax
import jax.numpy as jnp
import ml_dtypes
import numpy as np
from jax import lax
from jax.experimental import pallas as pl
from jax.experimental.pallas import tpu as pltpu
from jax.sharding import PartitionSpec as P

NX = 128
NY = 128
KX = 24
KY = 12
MODES = 288
C = 20
PL = 32
CP = C * PL
HP = 8
PART = C * HP
OUT_PARTS = 4
CR = 24
SCALE = 1.6656925
GROUP = ("gx", "gy")
BF = jnp.bfloat16
F32 = jnp.float32


def round_up(n, k):
    return -(-n // k) * k


def table(groups):
    per = MODES // groups
    rows = round_up(2 * per, 8)
    index = np.arange(KX)
    waves_x = np.where(index < KX // 2, index, NX - KX + index)
    kx = np.repeat(waves_x, KY)
    ky = np.tile(np.arange(KY), KX)
    x = np.arange(NX * NY) // NY
    y = np.arange(NX * NY) % NY
    turn = (kx[:, None] * x[None] + ky[:, None] * y[None]) % 128
    wheel = 2.0 * np.pi * np.arange(128) / 128
    both = np.stack([(SCALE * np.cos(wheel))[turn], (-SCALE * np.sin(wheel))[turn]], 0)
    both = both.reshape(2, groups, per, -1).transpose(1, 0, 2, 3).reshape(groups, 2 * per, -1)
    full = np.zeros((groups, rows, NX * NY), np.float32)
    full[:, : 2 * per] = both
    full = full.reshape(groups * rows, groups, -1).transpose(1, 0, 2)
    return full.astype(ml_dtypes.bfloat16)


def selectors(groups):
    per = MODES // groups
    rows = round_up(2 * per, 8)
    re, im = np.arange(per), per + np.arange(per)
    spread = np.zeros((rows, 256), np.float32)
    spread[re, re] = 1
    spread[im, im] = 1
    spread[im, 128 + re] = -1
    spread[re, 128 + im] = 1
    weights = np.zeros((per, 128), np.float32)
    weights[re, re] = 1
    weights[re, im] = 1
    collect = np.zeros((rows, 128), np.float32)
    collect[re, re] = 1
    collect[im, im] = 1
    fold = np.zeros((256, 256), np.float32)
    for first in (0, 128):
        fold[first + re, first + re] = 1
        fold[first + im, first + re] = 1
    cast = lambda a: a.astype(ml_dtypes.bfloat16)
    return (
        cast(np.concatenate([spread, spread], 0)),
        cast(weights),
        cast(np.concatenate([collect, collect], 1)),
        cast(np.concatenate([fold, fold], 0)),
    )


def plane_order():
    order = np.zeros((PL, CR, C, PL), np.float32)
    for d in range(C):
        order[np.arange(PL), d, d, np.arange(PL)] = 1
    return order.reshape(PL * CR, CP).astype(ml_dtypes.bfloat16)


def dot(a, b, ca, cb):
    return lax.dot_general(a, b, (((ca,), (cb,)), ((), ())), preferred_element_type=F32)


def encode(v):
    return ((v * jnp.abs(v)) * (v * v)).astype(BF)


def decode(y):
    return root(y.astype(F32))


def root(y):
    z = lax.rsqrt(jnp.maximum(jnp.abs(y), 1e-36))
    return ((y * z) * z) * lax.rsqrt(z)


def split(v):
    hi = v.astype(BF)
    return hi, (v - hi.astype(F32)).astype(BF)


def chunk_copies(pairs, parts, sem):
    copies = []
    for j in range(parts):
        copies.append([])
        for k, (source, target) in enumerate(pairs):
            width = target.shape[-1] // parts
            index = (slice(None),) * (len(target.shape) - 1) + (pl.ds(j * width, width),)
            copies[j].append(pltpu.make_async_copy(source.at[index], target.at[index], sem.at[k, j]))
    return copies


def start_chunk(copies, j):
    if j < len(copies):
        for copy in copies[j]:
            copy.start()


def first_kernel(groups, rows, parts, gid_ref, f_hbm, t_hbm, o_ref, f_ref, t_ref, acc_ref, sem):
    gid = gid_ref[0]
    width = f_ref.shape[1] // parts
    copies = chunk_copies([(f_hbm, f_ref), (t_hbm.at[gid], t_ref)], parts, sem)
    for j in range(parts):
        start_chunk(copies, j)
    for j in range(parts):
        at = slice(j * width, (j + 1) * width)
        for copy in copies[j]:
            copy.wait()
        part = dot(t_ref[:, at], f_ref[:, at], 1, 1)
        if j == 0:
            acc_ref[...] = part
        elif j < parts - 1:
            acc_ref[...] += part
    sent = acc_ref[...] + part if parts > 1 else part
    for g in range(groups):
        o_ref[g] = encode(sent[g * rows : (g + 1) * rows, :])


def same_plane(n):
    i = lax.broadcasted_iota(jnp.int32, (n, n), 0)
    j = lax.broadcasted_iota(jnp.int32, (n, n), 1)
    return lax.rem(i, HP) == lax.rem(j, HP)


def channel_of(lanes):
    i = lax.broadcasted_iota(jnp.int32, (PART, lanes), 0)
    j = lax.broadcasted_iota(jnp.int32, (PART, lanes), 1)
    return jnp.where(lax.div(i, HP) == j, 1.0, 0.0).astype(BF)


def planes_of(x, h):
    return x.reshape(C, PL // HP, HP, x.shape[1])[:, h].reshape(PART, x.shape[1])


def mix_kernel(
    groups, rows, cot_hbm, r_ref, w_ref, spread_ref, wsel_ref, collect_ref, v_ref, s_ref, cot_ref,
    wa_ref, wb_ref, vals_ref, sem,
):
    cot_copy = pltpu.make_async_copy(cot_hbm, cot_ref, sem.at[0])
    cot_copy.start()
    total = decode(r_ref[0])
    for g in range(1, groups):
        total = total + decode(r_ref[g])
    total = total * (1.0 / (SCALE * math.sqrt(NX * NY)))
    hi, lo = split(total)
    both = jnp.concatenate([hi.astype(F32), lo.astype(F32)], 0).astype(BF)
    s_ref[0, 0:CP, :] = dot(both, spread_ref[:, 0:128], 0, 0)
    s_ref[1, 0:CP, :] = dot(both, spread_ref[:, 128:256], 0, 0)
    s_ref[:, CP:, :] = jnp.zeros((2, CR * PL - CP, 128), F32)
    w = w_ref[...].astype(F32)
    wa_ref[...] = dot(w[:, 0, :].astype(BF), wsel_ref[...], 1, 0)
    wb_ref[...] = dot(w[:, 1, :].astype(BF), wsel_ref[...], 1, 0)

    def some(block, _):
        base = block * 4
        acc = [None] * 4
        for c in range(C):
            s = s_ref[0, c * PL : (c + 1) * PL, :]
            t = s_ref[1, c * PL : (c + 1) * PL, :]
            for k in range(4):
                row = c * C + base + k
                term = s * wa_ref[pl.ds(row, 1), :] + t * wb_ref[pl.ds(row, 1), :]
                acc[k] = term if acc[k] is None else acc[k] + term
        for k in range(4):
            vals_ref[pl.ds(pl.multiple_of((base + k) * PL, PL), PL), :] = acc[k]
        return 0

    lax.fori_loop(0, C // 4, some, 0)
    vals = vals_ref[...] * (1.0 / (SCALE * math.sqrt(MODES)))
    hi, lo = split(vals)
    v_ref[...] = dot(collect_ref[...], jnp.concatenate([hi, lo], 1), 1, 1).astype(BF)
    cot_copy.wait()


def gelu_both(h):
    k = math.sqrt(2.0 / math.pi)
    h2 = h * h
    t = jnp.tanh(h * (k + (k * 0.044715) * h2))
    half = 0.5 + 0.5 * t
    slope = half + (h * (half * (1.0 - t))) * (k + (3.0 * 0.044715 * k) * h2)
    return h * half, slope


def main_kernel(
    groups, rows, parts, t_ref, f_ref, cot_ref, v_ref, mix_ref, out_hbm, o_ref,
    out_ref, a_ref, acc_ref, product_ref, out_sem,
):
    width = f_ref.shape[1] // parts
    vals = jnp.transpose(v_ref[...].astype(F32))
    e = channel_of(C)
    m = jnp.where(same_plane(PART), dot(dot(e, mix_ref[...], 1, 1).astype(BF), e, 1, 1), 0.0)
    for h in range(PL // HP):
        a_ref[h] = jnp.concatenate([planes_of(vals, h), m], 1).astype(BF)
    out = []
    for j in range(parts):
        at = slice(j * width, (j + 1) * width)
        t = t_ref[:, at]
        f = f_ref[:, at].astype(F32)
        f = [planes_of(f, h).astype(BF) for h in range(PL // HP)]
        pre = [dot(a_ref[h], jnp.concatenate([t, f[h]], 0), 1, 0) for h in range(PL // HP)]
        pre = jnp.stack([x.reshape(C, HP, width) for x in pre], 1).reshape(CP, width)
        back = []
        for i in range(OUT_PARTS):
            some = slice(i * CP // OUT_PARTS, (i + 1) * CP // OUT_PARTS)
            value, slope = gelu_both(pre[some])
            out_ref[some, at] = value.astype(BF)
            out.append(pltpu.make_async_copy(out_ref.at[some, at], out_hbm.at[some, at], out_sem.at[j, i]))
            out[-1].start()
            back.append(cot_ref[some, at].astype(F32) * slope)
        back = jnp.concatenate(back, 0)
        part = dot(t, back.astype(BF), 1, 1)
        product = dot(f[0], planes_of(back, 0).astype(BF), 1, 1)
        for h in range(1, PL // HP):
            product = product + dot(f[h], planes_of(back, h).astype(BF), 1, 1)
        if j == 0:
            acc_ref[...] = part
            product_ref[...] = product
        else:
            acc_ref[...] += part
            product_ref[...] += product
    spectrum = acc_ref[...]
    product = product_ref[...]

    kept = jnp.where(same_plane(PART), product, 0.0)
    kept = jnp.sum(kept.reshape(C, HP, PART), axis=1)
    kept = jnp.concatenate([kept, jnp.zeros((CR - C, PART), F32)], 0)
    hi, lo = split(kept)
    e = channel_of(128)
    y = dot(hi, e, 1, 0) + dot(lo, e, 1, 0)
    yh = y.astype(BF).astype(F32)
    y = yh + pltpu.roll(y - yh, 64, 1)
    extra = y[0:8] + pltpu.roll(y[8:16], C, 1) + pltpu.roll(y[16:24], 2 * C, 1)
    for g in range(groups):
        v = spectrum[g * rows : (g + 1) * rows, :]
        coded = (v * jnp.abs(v)) * (v * v)
        tiles = [coded[:, 128 * i : 128 * (i + 1)] for i in range(CP // 128)]
        o_ref[g] = jnp.concatenate(tiles + [extra], 0).astype(BF)
    for copy in out:
        copy.wait()


def grad_kernel(groups, rows, per, r_ref, s_ref, spread_ref, fold_ref, order_ref, o_ref, g_ref, p_ref):
    high = rows * CP // 128
    total = None
    extra = None
    for g in range(groups):
        block = r_ref[g].astype(F32)
        y = root(block[0:high])
        total = y if total is None else total + y
        x = block[high : high + 8]
        extra = x if extra is None else extra + x
    total = total * (1.0 / (SCALE * math.sqrt(MODES)))
    total = jnp.concatenate([total[i * rows : (i + 1) * rows] for i in range(CP // 128)], 1)
    hi, lo = split(total)
    both = jnp.concatenate([hi.astype(F32), lo.astype(F32)], 0).astype(BF)
    hi, lo = split(dot(both, spread_ref[:, 0:128], 0, 0))
    by_plane = dot(order_ref[...], jnp.concatenate([hi, lo], 1), 1, 0)
    g_ref[...] = by_plane[:, 0:128] + by_plane[:, 128:256]

    for base in range(0, C, 4):
        one = [jnp.zeros((CR, 128), F32)] * 4
        two = [jnp.zeros((CR, 128), F32)] * 4
        for p in range(PL):
            g = g_ref[p * CR : (p + 1) * CR, :]
            for k in range(4):
                row = (base + k) * PL + p
                one[k] = one[k] + s_ref[0, row : row + 1, :] * g
                two[k] = two[k] + s_ref[1, row : row + 1, :] * g
        for k in range(4):
            at = (base + k) * CR
            p_ref[at : at + CR, 0:128] = one[k]
            p_ref[at : at + CR, 128:256] = two[k]
    products = jnp.concatenate([p_ref[c * CR : c * CR + C, :] for c in range(C)], 0)
    hi, lo = split(products)
    both = jnp.concatenate([hi, lo], 1)
    slots = dot(both, fold_ref[...], 1, 0)
    re, im = slots[:, 0:128], slots[:, 128:256]
    middle = pltpu.roll(jnp.concatenate([re[272:], im[0:144]], 0), per, 1)
    last = pltpu.roll(jnp.concatenate([im[144:], jnp.zeros((16, 128), F32)], 0), 2 * per, 1)
    lane = lax.broadcasted_iota(jnp.int32, (8, 128), 1)
    extra = extra + pltpu.roll(extra, 64, 1)
    pieces = []
    for k in range(3):
        piece = pltpu.roll(extra, (3 * per - k * C) % 128, 1)
        pieces.append(jnp.where(jnp.logical_and(lane >= 3 * per, lane < 3 * per + C), piece, 0.0))
    pieces.append(jnp.zeros((272 - 24, 128), F32))
    o_ref[...] = encode(re[0:272] + middle + last + jnp.concatenate(pieces, 0))


def last_kernel(per, samples, own_ref, other_ref, grad_ref, mix_ref):
    total = decode(own_ref[...]) + decode(other_ref[...])
    grads = total * (1.0 / math.sqrt(samples * PL))
    one = pltpu.roll(grads, 128 - per, 1)
    two = pltpu.roll(grads, 128 - 2 * per, 1)
    grad_ref[0:272, 0, :] = grads[:, 0:per]
    grad_ref[272:400, 0, :] = one[0:128, 0:per]
    grad_ref[0:144, 1, :] = one[128:272, 0:per]
    grad_ref[144:400, 1, :] = two[0:256, 0:per]
    mix = pltpu.roll(total[0:24], 128 - 3 * per, 1) * (1.0 / math.sqrt(samples * PL * NX * NY))
    mix_ref[...] = mix[0:C, 0:C]


def sum_over_dp(coded, samples):
    if samples & (samples - 1) or samples == 1:
        total = jnp.sum(decode(lax.all_gather(coded, "dp", axis=0)), axis=0)
        return encode(total), jnp.zeros_like(coded)
    step = 1
    while True:
        other = lax.ppermute(coded, "dp", [(i, i ^ step) for i in range(samples)])
        step *= 2
        if step >= samples:
            return coded, other
        coded = encode(decode(coded) + decode(other))


def compiler_params(mib):
    return pltpu.CompilerParams(vmem_limit_bytes=mib * 2**20)


def local(tables, consts, fields, cotangent, mix_weight, spectral_weight):
    spread, wsel, collect, fold = consts
    cells = fields.shape[3]
    groups = lax.axis_size("gx") * lax.axis_size("gy")
    samples = lax.axis_size("dp")
    per = MODES // groups
    rows = round_up(2 * per, 8)
    flat = fields.reshape(CP, cells)
    cot = cotangent.reshape(CP, cells)
    gid = (lax.axis_index("gx") * lax.axis_size("gy") + lax.axis_index("gy")).astype(jnp.int32).reshape(1)
    halves = max(1, cells // 1024)
    high = groups * rows
    vmem = pl.BlockSpec(memory_space=pltpu.VMEM)
    smem = pl.BlockSpec(memory_space=pltpu.SMEM)

    hbm = pl.BlockSpec(memory_space=pltpu.HBM)

    sent, flat_in, table_in = pl.pallas_call(
        functools.partial(first_kernel, groups, rows, halves),
        in_specs=[smem, hbm, hbm],
        out_specs=(vmem, vmem, vmem),
        out_shape=(
            jax.ShapeDtypeStruct((groups, rows, CP), BF),
            jax.ShapeDtypeStruct((CP, cells), BF),
            jax.ShapeDtypeStruct((high, cells), BF),
        ),
        scratch_shapes=[
            pltpu.VMEM((high, CP), F32),
            pltpu.SemaphoreType.DMA((2, halves)),
        ],
        compiler_params=compiler_params(50),
        name="spectrum_parts",
    )(gid, flat, tables)
    got = lax.all_to_all(sent, GROUP, 0, 0, tiled=True)

    weights = jnp.transpose(spectral_weight, (2, 3, 1, 0)).reshape(C * C, 2, per)
    vals, spec, cot_in = pl.pallas_call(
        functools.partial(mix_kernel, groups, rows),
        in_specs=[hbm] + [vmem] * 5,
        out_specs=[vmem] * 3,
        out_shape=[
            jax.ShapeDtypeStruct((rows, CP), BF),
            jax.ShapeDtypeStruct((2, CR * PL, 128), F32),
            jax.ShapeDtypeStruct((CP, cells), BF),
        ],
        scratch_shapes=[
            pltpu.VMEM((C * C, 128), F32),
            pltpu.VMEM((C * C, 128), F32),
            pltpu.VMEM((CP, 128), F32),
            pltpu.SemaphoreType.DMA((1,)),
        ],
        compiler_params=compiler_params(48),
        name="mode_mixing",
    )(cot, got, weights, spread, wsel, collect)
    all_vals = lax.all_gather(vals, GROUP, axis=0, tiled=True)

    output, sent = pl.pallas_call(
        functools.partial(main_kernel, groups, rows, 1),
        in_specs=[vmem] * 5,
        out_specs=(hbm, vmem),
        out_shape=(
            jax.ShapeDtypeStruct((CP, cells), BF),
            jax.ShapeDtypeStruct((groups, rows * CP // 128 + 8, 128), BF),
        ),
        scratch_shapes=[
            pltpu.VMEM((CP, cells), BF),
            pltpu.VMEM((PL // HP, PART, high + PART), BF),
            pltpu.VMEM((high, CP), F32),
            pltpu.VMEM((PART, PART), F32),
            pltpu.SemaphoreType.DMA((1, OUT_PARTS)),
        ],
        compiler_params=compiler_params(40),
        name="cells",
    )(table_in, flat_in, cot_in, all_vals, mix_weight)
    got = lax.all_to_all(sent, GROUP, 0, 0, tiled=True)

    coded = pl.pallas_call(
        functools.partial(grad_kernel, groups, rows, per),
        out_shape=jax.ShapeDtypeStruct((272, 128), BF),
        scratch_shapes=[pltpu.VMEM((CR * PL, 128), F32), pltpu.VMEM((C * CR, 256), F32)],
        compiler_params=compiler_params(8),
        name="mode_grads",
    )(got, spec, spread, fold, plane_order())
    own, other = sum_over_dp(coded, samples)
    grads, mixing_grad = pl.pallas_call(
        functools.partial(last_kernel, per, samples),
        out_shape=(jax.ShapeDtypeStruct((C * C, 2, per), F32), jax.ShapeDtypeStruct((C, C), F32)),
        compiler_params=compiler_params(8),
        name="gradients_out",
    )(own, other)
    spectral_grad = jnp.transpose(grads.reshape(C, C, 2, per), (3, 2, 0, 1))
    return (output.reshape(1, C, PL, cells), spectral_grad, mixing_grad)


def solution(mesh):
    groups = mesh.shape["gx"] * mesh.shape["gy"]
    body = functools.partial(local, table(groups), selectors(groups))
    return jax.shard_map(
        body,
        mesh=mesh,
        in_specs=(
            P("dp", None, None, GROUP),
            P("dp", None, None, GROUP),
            P(),
            P(GROUP, None, None, None),
        ),
        out_specs=(P("dp", None, None, GROUP), P(GROUP, None, None, None), P()),
        check_vma=False,
    )
```

```python
import functools
import math

import jax
import jax.numpy as jnp
import ml_dtypes
import numpy as np
from jax import lax
from jax.experimental import pallas as pl
from jax.experimental.pallas import tpu as pltpu
from jax.sharding import PartitionSpec as P

NX = 128
NY = 128
KX = 24
KY = 12
MODES = 288
C = 20
PL = 32
CP = C * PL
HP = 8
PART = C * HP
OUT_PARTS = 4
ROWS = 240
CR = 24
SCALE = 1.6656925
GROUP = ("gx", "gy")
BF = jnp.bfloat16
F32 = jnp.float32


def round_up(n, k):
    return -(-n // k) * k


def table(groups):
    per = MODES // groups
    rows = round_up(2 * per, 8)
    index = np.arange(KX)
    waves_x = np.where(index < KX // 2, index, NX - KX + index)
    kx = np.repeat(waves_x, KY)
    ky = np.tile(np.arange(KY), KX)
    x = np.arange(NX * NY) // NY
    y = np.arange(NX * NY) % NY
    turn = (kx[:, None] * x[None] + ky[:, None] * y[None]) % 128
    wheel = 2.0 * np.pi * np.arange(128) / 128
    both = np.stack([(SCALE * np.cos(wheel))[turn], (-SCALE * np.sin(wheel))[turn]], 0)
    both = both.reshape(2, groups, per, -1).transpose(1, 0, 2, 3).reshape(groups, 2 * per, -1)
    full = np.zeros((groups, rows, NX * NY), np.float32)
    full[:, : 2 * per] = both
    full = full.reshape(groups * rows, groups, -1).transpose(1, 0, 2)
    return full.astype(ml_dtypes.bfloat16)


def selectors(groups):
    per = MODES // groups
    rows = round_up(2 * per, 8)
    re, im = np.arange(per), per + np.arange(per)
    spread = np.zeros((rows, 256), np.float32)
    spread[re, re] = 1
    spread[im, im] = 1
    spread[im, 128 + re] = -1
    spread[re, 128 + im] = 1
    weights = np.zeros((per, 128), np.float32)
    weights[re, re] = 1
    weights[re, im] = 1
    collect = np.zeros((rows, 128), np.float32)
    collect[re, re] = 1
    collect[im, im] = 1
    fold = np.zeros((256, 256), np.float32)
    for first in (0, 128):
        fold[first + re, first + re] = 1
        fold[first + im, first + re] = 1
    cast = lambda a: a.astype(ml_dtypes.bfloat16)
    return (
        cast(np.concatenate([spread, spread], 0)),
        cast(weights),
        cast(np.concatenate([collect, collect], 1)),
        cast(np.concatenate([fold, fold], 0)),
    )


def plane_order():
    order = np.zeros((PL, CR, C, PL), np.float32)
    for d in range(C):
        order[np.arange(PL), d, d, np.arange(PL)] = 1
    return order.reshape(PL * CR, CP).astype(ml_dtypes.bfloat16)


def dot(a, b, ca, cb):
    return lax.dot_general(a, b, (((ca,), (cb,)), ((), ())), preferred_element_type=F32)


def encode(v):
    return ((v * jnp.abs(v)) * (v * v)).astype(BF)


def decode(y):
    return root(y.astype(F32))


def root(y):
    z = lax.rsqrt(jnp.maximum(jnp.abs(y), 1e-36))
    return ((y * z) * z) * lax.rsqrt(z)


def split(v):
    hi = v.astype(BF)
    return hi, (v - hi.astype(F32)).astype(BF)


def chunk_copies(pairs, parts, sem):
    copies = []
    for j in range(parts):
        copies.append([])
        for k, (source, target) in enumerate(pairs):
            width = target.shape[-1] // parts
            index = (slice(None),) * (len(target.shape) - 1) + (pl.ds(j * width, width),)
            copies[j].append(pltpu.make_async_copy(source.at[index], target.at[index], sem.at[k, j]))
    return copies


def start_chunk(copies, j):
    if j < len(copies):
        for copy in copies[j]:
            copy.start()


def first_kernel(groups, rows, parts, gid_ref, f_hbm, t_hbm, o_ref, f_ref, t_ref, acc_ref, sem):
    gid = gid_ref[0]
    width = f_ref.shape[1] // parts
    copies = chunk_copies([(f_hbm, f_ref), (t_hbm.at[gid], t_ref)], parts, sem)
    for j in range(parts):
        start_chunk(copies, j)
    for j in range(parts):
        at = slice(j * width, (j + 1) * width)
        for copy in copies[j]:
            copy.wait()
        part = dot(t_ref[:, at], f_ref[:, at], 1, 1)
        if j == 0:
            acc_ref[...] = part
        elif j < parts - 1:
            acc_ref[...] += part
    sent = acc_ref[...] + part if parts > 1 else part
    for g in range(groups):
        o_ref[g] = encode(sent[g * rows : (g + 1) * rows, :])


def same_plane(n):
    i = lax.broadcasted_iota(jnp.int32, (n, n), 0)
    j = lax.broadcasted_iota(jnp.int32, (n, n), 1)
    return lax.rem(i, HP) == lax.rem(j, HP)


def channel_of(lanes):
    i = lax.broadcasted_iota(jnp.int32, (PART, lanes), 0)
    j = lax.broadcasted_iota(jnp.int32, (PART, lanes), 1)
    return jnp.where(lax.div(i, HP) == j, 1.0, 0.0).astype(BF)


def planes_of(x, h):
    return x.reshape(C, PL // HP, HP, x.shape[1])[:, h].reshape(PART, x.shape[1])


def mix_kernel(
    groups, rows, cot_hbm, r_ref, w_ref, spread_ref, wsel_ref, collect_ref, v_ref, s_ref, cot_ref,
    wa_ref, wb_ref, vals_ref, sem,
):
    cot_copy = pltpu.make_async_copy(cot_hbm, cot_ref, sem.at[0])
    cot_copy.start()
    total = decode(r_ref[0])
    for g in range(1, groups):
        total = total + decode(r_ref[g])
    total = total * (1.0 / (SCALE * math.sqrt(NX * NY)))
    hi, lo = split(total)
    both = jnp.concatenate([hi.astype(F32), lo.astype(F32)], 0).astype(BF)
    s_ref[0, 0:CP, :] = dot(both, spread_ref[:, 0:128], 0, 0)
    s_ref[1, 0:CP, :] = dot(both, spread_ref[:, 128:256], 0, 0)
    s_ref[:, CP:, :] = jnp.zeros((2, CR * PL - CP, 128), F32)
    w = w_ref[...].astype(F32)
    wa_ref[...] = dot(w[:, 0, :].astype(BF), wsel_ref[...], 1, 0)
    wb_ref[...] = dot(w[:, 1, :].astype(BF), wsel_ref[...], 1, 0)

    def some(block, _):
        base = block * 4
        acc = [None] * 4
        for c in range(C):
            s = s_ref[0, c * PL : (c + 1) * PL, :]
            t = s_ref[1, c * PL : (c + 1) * PL, :]
            for k in range(4):
                row = c * C + base + k
                term = s * wa_ref[pl.ds(row, 1), :] + t * wb_ref[pl.ds(row, 1), :]
                acc[k] = term if acc[k] is None else acc[k] + term
        for k in range(4):
            vals_ref[pl.ds(pl.multiple_of((base + k) * PL, PL), PL), :] = acc[k]
        return 0

    lax.fori_loop(0, C // 4, some, 0)
    vals = vals_ref[...] * (1.0 / (SCALE * math.sqrt(MODES)))
    hi, lo = split(vals)
    v_ref[...] = dot(collect_ref[...], jnp.concatenate([hi, lo], 1), 1, 1).astype(BF)
    cot_copy.wait()


def gelu_both(h):
    k = math.sqrt(2.0 / math.pi)
    h2 = h * h
    t = jnp.tanh(h * (k + (k * 0.044715) * h2))
    half = 0.5 + 0.5 * t
    slope = half + (h * (half * (1.0 - t))) * (k + (3.0 * 0.044715 * k) * h2)
    return h * half, slope


def main_kernel(
    groups, rows, parts, t_ref, f_ref, cot_ref, v_ref, mix_ref, out_hbm, o_ref,
    out_ref, a_ref, acc_ref, product_ref, out_sem,
):
    width = f_ref.shape[1] // parts
    vals = jnp.transpose(v_ref[...].astype(F32))
    e = channel_of(C)
    m = jnp.where(same_plane(PART), dot(dot(e, mix_ref[...], 1, 1).astype(BF), e, 1, 1), 0.0)
    for h in range(PL // HP):
        a_ref[h] = jnp.concatenate([planes_of(vals, h), m], 1).astype(BF)
    out = []
    for j in range(parts):
        at = slice(j * width, (j + 1) * width)
        t = t_ref[:, at]
        f = f_ref[:, at].astype(F32)
        f = [planes_of(f, h).astype(BF) for h in range(PL // HP)]
        pre = [dot(a_ref[h], jnp.concatenate([t, f[h]], 0), 1, 0) for h in range(PL // HP)]
        pre = jnp.stack([x.reshape(C, HP, width) for x in pre], 1).reshape(CP, width)
        back = []
        for i in range(OUT_PARTS):
            some = slice(i * CP // OUT_PARTS, (i + 1) * CP // OUT_PARTS)
            value, slope = gelu_both(pre[some])
            out_ref[some, at] = value.astype(BF)
            out.append(pltpu.make_async_copy(out_ref.at[some, at], out_hbm.at[some, at], out_sem.at[j, i]))
            out[-1].start()
            back.append(cot_ref[some, at].astype(F32) * slope)
        back = jnp.concatenate(back, 0)
        part = dot(t, back.astype(BF), 1, 1)
        product = dot(f[0], planes_of(back, 0).astype(BF), 1, 1)
        for h in range(1, PL // HP):
            product = product + dot(f[h], planes_of(back, h).astype(BF), 1, 1)
        if j == 0:
            acc_ref[...] = part
            product_ref[...] = product
        else:
            acc_ref[...] += part
            product_ref[...] += product
    spectrum = acc_ref[...]
    product = product_ref[...]

    kept = jnp.where(same_plane(PART), product, 0.0)
    kept = jnp.sum(kept.reshape(C, HP, PART), axis=1)
    kept = jnp.concatenate([kept, jnp.zeros((CR - C, PART), F32)], 0)
    hi, lo = split(kept)
    e = channel_of(128)
    y = dot(hi, e, 1, 0) + dot(lo, e, 1, 0)
    yh = y.astype(BF).astype(F32)
    y = yh + pltpu.roll(y - yh, 64, 1)
    extra = y[0:8] + pltpu.roll(y[8:16], C, 1) + pltpu.roll(y[16:24], 2 * C, 1)
    for g in range(groups):
        v = spectrum[g * rows : (g + 1) * rows, :]
        coded = (v * jnp.abs(v)) * (v * v)
        tiles = [coded[:, 128 * i : 128 * (i + 1)] for i in range(CP // 128)]
        o_ref[g] = jnp.concatenate(tiles + [extra], 0).astype(BF)
    for copy in out:
        copy.wait()


def grad_kernel(groups, rows, per, r_ref, s_ref, spread_ref, fold_ref, order_ref, o_ref, g_ref, p_ref):
    high = rows * CP // 128
    total = None
    extra = None
    for g in range(groups):
        block = r_ref[g].astype(F32)
        y = root(block[0:high])
        total = y if total is None else total + y
        x = block[high : high + 8]
        extra = x if extra is None else extra + x
    total = total * (1.0 / (SCALE * math.sqrt(MODES)))
    total = jnp.concatenate([total[i * rows : (i + 1) * rows] for i in range(CP // 128)], 1)
    hi, lo = split(total)
    both = jnp.concatenate([hi.astype(F32), lo.astype(F32)], 0).astype(BF)
    hi, lo = split(dot(both, spread_ref[:, 0:128], 0, 0))
    by_plane = dot(order_ref[...], jnp.concatenate([hi, lo], 1), 1, 0)
    g_ref[...] = by_plane[:, 0:128] + by_plane[:, 128:256]

    for base in range(0, C, 4):
        one = [jnp.zeros((CR, 128), F32)] * 4
        two = [jnp.zeros((CR, 128), F32)] * 4
        for p in range(PL):
            g = g_ref[p * CR : (p + 1) * CR, :]
            for k in range(4):
                row = (base + k) * PL + p
                one[k] = one[k] + s_ref[0, row : row + 1, :] * g
                two[k] = two[k] + s_ref[1, row : row + 1, :] * g
        for k in range(4):
            at = (base + k) * CR
            p_ref[at : at + CR, 0:128] = one[k]
            p_ref[at : at + CR, 128:256] = two[k]
    products = jnp.concatenate([p_ref[c * CR : c * CR + C, :] for c in range(C)], 0)
    hi, lo = split(products)
    both = jnp.concatenate([hi, lo], 1)
    slots = dot(both, fold_ref[...], 1, 0)
    re, im = slots[:, 0:128], slots[:, 128:256]
    lane = lax.broadcasted_iota(jnp.int32, (8, 128), 1)
    extra = extra + pltpu.roll(extra, 64, 1)
    slot = [im[320:], pltpu.roll(im[320:], 128 - C, 1)]
    slot += [extra if k == 0 else pltpu.roll(extra, 128 - k * C, 1) for k in range(3)]
    slot = jnp.concatenate(slot + [jnp.zeros((ROWS - 184, 128), F32)], 0)
    narrow = lax.broadcasted_iota(jnp.int32, (ROWS, 128), 1) < C
    payload = re[0:ROWS] + pltpu.roll(jnp.concatenate([re[ROWS:], im[0:80]], 0), per, 1)
    payload = payload + pltpu.roll(im[80:320], 2 * per, 1)
    o_ref[...] = encode(payload + pltpu.roll(jnp.where(narrow, slot, 0.0), 3 * per, 1))


def last_kernel(per, samples, *refs):
    parts, (grad_ref, mix_ref) = [decode(ref[...]) for ref in refs[:-2]], refs[-2:]
    total = parts[0] + parts[1]
    if len(parts) == 4:
        total = total + (parts[2] + parts[3])
    grads = total * (1.0 / math.sqrt(samples * PL))
    one = pltpu.roll(grads, 128 - per, 1)
    two = pltpu.roll(grads, 128 - 2 * per, 1)
    slot = pltpu.roll(total, 128 - 3 * per, 1)
    grad_ref[0:240, 0, :] = grads[:, 0:per]
    grad_ref[240:400, 0, :] = one[0:160, 0:per]
    grad_ref[0:80, 1, :] = one[160:240, 0:per]
    grad_ref[80:320, 1, :] = two[:, 0:per]
    narrow = lax.broadcasted_iota(jnp.int32, (80, 128), 1) < C
    rest = jnp.where(narrow, slot[0:80], pltpu.roll(slot[80:160], C, 1)) * (1.0 / math.sqrt(samples * PL))
    grad_ref[320:400, 1, :] = rest[:, 0:per]
    mix_ref[...] = slot[160 : 160 + C, 0:C] * (1.0 / math.sqrt(samples * PL * NX * NY))


def sum_over_dp(coded, samples):
    if samples & (samples - 1) or samples == 1:
        total = jnp.sum(decode(lax.all_gather(coded, "dp", axis=0)), axis=0)
        return encode(total), jnp.zeros_like(coded)
    if samples == 4:
        return [coded] + [lax.ppermute(coded, "dp", [(i, i ^ k) for i in range(samples)]) for k in range(1, samples)]
    step = 1
    while True:
        other = lax.ppermute(coded, "dp", [(i, i ^ step) for i in range(samples)])
        step *= 2
        if step >= samples:
            return coded, other
        coded = encode(decode(coded) + decode(other))


def compiler_params(mib):
    return pltpu.CompilerParams(vmem_limit_bytes=mib * 2**20)


def local(tables, consts, fields, cotangent, mix_weight, spectral_weight):
    spread, wsel, collect, fold = consts
    cells = fields.shape[3]
    groups = lax.axis_size("gx") * lax.axis_size("gy")
    samples = lax.axis_size("dp")
    per = MODES // groups
    rows = round_up(2 * per, 8)
    flat = fields.reshape(CP, cells)
    cot = cotangent.reshape(CP, cells)
    gid = (lax.axis_index("gx") * lax.axis_size("gy") + lax.axis_index("gy")).astype(jnp.int32).reshape(1)
    halves = max(1, cells // 1024)
    high = groups * rows
    vmem = pl.BlockSpec(memory_space=pltpu.VMEM)
    smem = pl.BlockSpec(memory_space=pltpu.SMEM)

    hbm = pl.BlockSpec(memory_space=pltpu.HBM)

    sent, flat_in, table_in = pl.pallas_call(
        functools.partial(first_kernel, groups, rows, halves),
        in_specs=[smem, hbm, hbm],
        out_specs=(vmem, vmem, vmem),
        out_shape=(
            jax.ShapeDtypeStruct((groups, rows, CP), BF),
            jax.ShapeDtypeStruct((CP, cells), BF),
            jax.ShapeDtypeStruct((high, cells), BF),
        ),
        scratch_shapes=[
            pltpu.VMEM((high, CP), F32),
            pltpu.SemaphoreType.DMA((2, halves)),
        ],
        compiler_params=compiler_params(50),
        name="spectrum_parts",
    )(gid, flat, tables)
    got = lax.all_to_all(sent, GROUP, 0, 0, tiled=True)

    weights = jnp.transpose(spectral_weight, (2, 3, 1, 0)).reshape(C * C, 2, per)
    vals, spec, cot_in = pl.pallas_call(
        functools.partial(mix_kernel, groups, rows),
        in_specs=[hbm] + [vmem] * 5,
        out_specs=[vmem] * 3,
        out_shape=[
            jax.ShapeDtypeStruct((rows, CP), BF),
            jax.ShapeDtypeStruct((2, CR * PL, 128), F32),
            jax.ShapeDtypeStruct((CP, cells), BF),
        ],
        scratch_shapes=[
            pltpu.VMEM((C * C, 128), F32),
            pltpu.VMEM((C * C, 128), F32),
            pltpu.VMEM((CP, 128), F32),
            pltpu.SemaphoreType.DMA((1,)),
        ],
        compiler_params=compiler_params(48),
        name="mode_mixing",
    )(cot, got, weights, spread, wsel, collect)
    all_vals = lax.all_gather(vals, GROUP, axis=0, tiled=True)

    output, sent = pl.pallas_call(
        functools.partial(main_kernel, groups, rows, 1),
        in_specs=[vmem] * 5,
        out_specs=(hbm, vmem),
        out_shape=(
            jax.ShapeDtypeStruct((CP, cells), BF),
            jax.ShapeDtypeStruct((groups, rows * CP // 128 + 8, 128), BF),
        ),
        scratch_shapes=[
            pltpu.VMEM((CP, cells), BF),
            pltpu.VMEM((PL // HP, PART, high + PART), BF),
            pltpu.VMEM((high, CP), F32),
            pltpu.VMEM((PART, PART), F32),
            pltpu.SemaphoreType.DMA((1, OUT_PARTS)),
        ],
        compiler_params=compiler_params(40),
        name="cells",
    )(table_in, flat_in, cot_in, all_vals, mix_weight)
    got = lax.all_to_all(sent, GROUP, 0, 0, tiled=True)

    coded = pl.pallas_call(
        functools.partial(grad_kernel, groups, rows, per),
        out_shape=jax.ShapeDtypeStruct((ROWS, 128), BF),
        scratch_shapes=[pltpu.VMEM((CR * PL, 128), F32), pltpu.VMEM((C * CR, 256), F32)],
        compiler_params=compiler_params(8),
        name="mode_grads",
    )(got, spec, spread, fold, plane_order())
    summands = sum_over_dp(coded, samples)
    grads, mixing_grad = pl.pallas_call(
        functools.partial(last_kernel, per, samples),
        out_shape=(jax.ShapeDtypeStruct((C * C, 2, per), F32), jax.ShapeDtypeStruct((C, C), F32)),
        compiler_params=compiler_params(8),
        name="gradients_out",
    )(*summands)
    spectral_grad = jnp.transpose(grads.reshape(C, C, 2, per), (3, 2, 0, 1))
    return (output.reshape(1, C, PL, cells), spectral_grad, mixing_grad)


def solution(mesh):
    groups = mesh.shape["gx"] * mesh.shape["gy"]
    body = functools.partial(local, table(groups), selectors(groups))
    return jax.shard_map(
        body,
        mesh=mesh,
        in_specs=(
            P("dp", None, None, GROUP),
            P("dp", None, None, GROUP),
            P(),
            P(GROUP, None, None, None),
        ),
        out_specs=(P("dp", None, None, GROUP), P(GROUP, None, None, None), P()),
        check_vma=False,
    )
```

```python
import functools
import math

import jax
import jax.numpy as jnp
import ml_dtypes
import numpy as np
from jax import lax
from jax.experimental import pallas as pl
from jax.experimental.pallas import tpu as pltpu
from jax.sharding import PartitionSpec as P

NX = 128
NY = 128
KX = 24
KY = 12
MODES = 288
C = 20
PL = 32
CP = C * PL
HP = 8
PART = C * HP
OUT_PARTS = 4
MAIN = 32
ROWS = 240
CR = 24
SCALE = 1.6656925
GROUP = ("gx", "gy")
BF = jnp.bfloat16
F32 = jnp.float32


def round_up(n, k):
    return -(-n // k) * k


def table(groups):
    per = MODES // groups
    rows = round_up(2 * per, 8)
    index = np.arange(KX)
    waves_x = np.where(index < KX // 2, index, NX - KX + index)
    kx = np.repeat(waves_x, KY)
    ky = np.tile(np.arange(KY), KX)
    x = np.arange(NX * NY) // NY
    y = np.arange(NX * NY) % NY
    turn = (kx[:, None] * x[None] + ky[:, None] * y[None]) % 128
    wheel = 2.0 * np.pi * np.arange(128) / 128
    both = np.stack([(SCALE * np.cos(wheel))[turn], (-SCALE * np.sin(wheel))[turn]], 0)
    both = both.reshape(2, groups, per, -1).transpose(1, 0, 2, 3).reshape(groups, 2 * per, -1)
    full = np.zeros((groups, rows, NX * NY), np.float32)
    full[:, : 2 * per] = both
    full = full.reshape(groups * rows, groups, -1).transpose(1, 0, 2)
    return full.astype(ml_dtypes.bfloat16)


def selectors(groups):
    per = MODES // groups
    rows = round_up(2 * per, 8)
    re, im = np.arange(per), per + np.arange(per)
    main = min(per, MAIN)
    pairs = np.zeros((rows, 512), np.float32)
    weights = np.zeros((2, per, 256), np.float32)
    collect = np.zeros((rows, 256), np.float32)
    fold = np.zeros((256, 256), np.float32)
    for k, (s_row, s_sign, g_row) in enumerate(((re, 1, re), (im, 1, im), (im, -1, re), (re, 1, im))):
        for m in range(per):
            places = [k * MAIN + m] if m < main else [128 + 16 * j + 4 * k + m - main for j in range(8)]
            for at in places:
                pairs[s_row[m], at] = s_sign
                pairs[g_row[m], 256 + at] = 1
                fold[at, 128 * (k // 2) + m] = 1
                weights[k // 2, m, at] = 1
                collect[(re, im)[k % 2][m], at] = 1
    cast = lambda a: a.astype(ml_dtypes.bfloat16)
    return (
        cast(weights),
        cast(np.concatenate([collect, collect], 1)),
        cast(np.concatenate([fold, fold], 0)),
        cast(np.concatenate([pairs, pairs], 0)),
    )


def plane_order():
    order = np.zeros((PL, CR, C, PL), np.float32)
    for d in range(C):
        order[np.arange(PL), d, d, np.arange(PL)] = 1
    return order.reshape(PL * CR, CP).astype(ml_dtypes.bfloat16)


def dot(a, b, ca, cb):
    return lax.dot_general(a, b, (((ca,), (cb,)), ((), ())), preferred_element_type=F32)


def encode(v):
    return ((v * jnp.abs(v)) * (v * v)).astype(BF)


def decode(y):
    return root(y.astype(F32))


def root(y):
    z = lax.rsqrt(jnp.maximum(jnp.abs(y), 1e-36))
    return ((y * z) * z) * lax.rsqrt(z)


def split(v):
    hi = v.astype(BF)
    return hi, (v - hi.astype(F32)).astype(BF)


def chunk_copies(pairs, parts, sem):
    copies = []
    for j in range(parts):
        copies.append([])
        for k, (source, target) in enumerate(pairs):
            width = target.shape[-1] // parts
            index = (slice(None),) * (len(target.shape) - 1) + (pl.ds(j * width, width),)
            copies[j].append(pltpu.make_async_copy(source.at[index], target.at[index], sem.at[k, j]))
    return copies


def start_chunk(copies, j):
    if j < len(copies):
        for copy in copies[j]:
            copy.start()


def first_kernel(groups, rows, parts, gid_ref, f_hbm, t_hbm, o_ref, f_ref, t_ref, acc_ref, sem):
    gid = gid_ref[0]
    width = f_ref.shape[1] // parts
    copies = chunk_copies([(f_hbm, f_ref), (t_hbm.at[gid], t_ref)], parts, sem)
    for j in range(parts):
        start_chunk(copies, j)
    for j in range(parts):
        at = slice(j * width, (j + 1) * width)
        for copy in copies[j]:
            copy.wait()
        part = dot(t_ref[:, at], f_ref[:, at], 1, 1)
        if j == 0:
            acc_ref[...] = part
        elif j < parts - 1:
            acc_ref[...] += part
    sent = acc_ref[...] + part if parts > 1 else part
    for g in range(groups):
        o_ref[g] = encode(sent[g * rows : (g + 1) * rows, :])


def same_plane(n):
    i = lax.broadcasted_iota(jnp.int32, (n, n), 0)
    j = lax.broadcasted_iota(jnp.int32, (n, n), 1)
    return lax.rem(i, HP) == lax.rem(j, HP)


def channel_of(lanes):
    i = lax.broadcasted_iota(jnp.int32, (PART, lanes), 0)
    j = lax.broadcasted_iota(jnp.int32, (PART, lanes), 1)
    return jnp.where(lax.div(i, HP) == j, 1.0, 0.0).astype(BF)


def planes_of(x, h):
    return x.reshape(C, PL // HP, HP, x.shape[1])[:, h].reshape(PART, x.shape[1])


def own_group():
    shape = (PL // 8, 8, 128)
    group = 2 * lax.broadcasted_iota(jnp.int32, shape, 0) + lax.div(lax.broadcasted_iota(jnp.int32, shape, 1), 4)
    return group == lax.div(lax.broadcasted_iota(jnp.int32, shape, 2), 16)


def across_lanes(x):
    x = jnp.where(own_group()[None], x.reshape(C, PL // 8, 8, 128), 0.0)
    x = jnp.sum(x, axis=1)
    return (x + jnp.concatenate([x[:, 4:], x[:, :4]], 1)).reshape(C * 8, 128)


def along_planes(x):
    return jnp.where(own_group()[None], x.reshape(C, 1, 8, 128), 0.0).reshape(CP, 128)


def mix_kernel(
    groups, rows, per, cot_hbm, r_ref, w_ref, wsel_ref, collect_ref, pairs_ref,
    v_ref, spec_ref, spec_rest_ref, cot_ref, weights_ref, vals_ref, rest_ref, sem,
):
    cot_copy = pltpu.make_async_copy(cot_hbm, cot_ref, sem.at[0])
    cot_copy.start()
    total = decode(r_ref[0])
    for g in range(1, groups):
        total = total + decode(r_ref[g])
    total = total * (1.0 / (SCALE * math.sqrt(NX * NY)))
    hi, lo = split(total)
    both = jnp.concatenate([hi.astype(F32), lo.astype(F32)], 0).astype(BF)
    spec_ref[...] = dot(both, pairs_ref[:, 0:128], 0, 0)
    spec_rest_ref[...] = across_lanes(dot(both, pairs_ref[:, 128:256], 0, 0))
    w = w_ref[...].astype(F32)
    weights_ref[...] = dot(w[:, 0, :].astype(BF), wsel_ref[0], 1, 0) + dot(w[:, 1, :].astype(BF), wsel_ref[1], 1, 0)

    for base in range(0, C, 4):
        main = [None] * 4
        rest = [None] * 4
        for c in range(C):
            s = spec_ref[c * PL : (c + 1) * PL, :]
            t = spec_rest_ref[c * 8 : (c + 1) * 8, :]
            for k in range(4):
                row = c * C + base + k
                one = s * weights_ref[row : row + 1, 0:128]
                main[k] = one if main[k] is None else main[k] + one
                two = t * weights_ref[row : row + 1, 128:256]
                rest[k] = two if rest[k] is None else rest[k] + two
        for k in range(4):
            d = base + k
            vals_ref[d * PL : (d + 1) * PL, :] = main[k]
            rest_ref[d * 8 : (d + 1) * 8, :] = rest[k]
    vals = jnp.concatenate([vals_ref[...], along_planes(rest_ref[...])], 1)
    hi, lo = split(vals * (1.0 / (SCALE * math.sqrt(MODES))))
    v_ref[...] = dot(collect_ref[...], jnp.concatenate([hi, lo], 1), 1, 1).astype(BF)
    cot_copy.wait()


def gelu_both(h):
    k = math.sqrt(2.0 / math.pi)
    h2 = h * h
    t = jnp.tanh(h * (k + (k * 0.044715) * h2))
    half = 0.5 + 0.5 * t
    slope = half + (h * (half * (1.0 - t))) * (k + (3.0 * 0.044715 * k) * h2)
    return h * half, slope


def main_kernel(
    groups, rows, parts, t_ref, f_ref, cot_ref, v_ref, mix_ref, out_hbm, o_ref,
    out_ref, a_ref, acc_ref, product_ref, out_sem,
):
    width = f_ref.shape[1] // parts
    vals = jnp.transpose(v_ref[...].astype(F32))
    e = channel_of(C)
    m = jnp.where(same_plane(PART), dot(dot(e, mix_ref[...], 1, 1).astype(BF), e, 1, 1), 0.0)
    for h in range(PL // HP):
        a_ref[h] = jnp.concatenate([planes_of(vals, h), m], 1).astype(BF)
    out = []
    for j in range(parts):
        at = slice(j * width, (j + 1) * width)
        t = t_ref[:, at]
        f = f_ref[:, at].astype(F32)
        f = [planes_of(f, h).astype(BF) for h in range(PL // HP)]
        pre = [dot(a_ref[h], jnp.concatenate([t, f[h]], 0), 1, 0) for h in range(PL // HP)]
        pre = jnp.stack([x.reshape(C, HP, width) for x in pre], 1).reshape(CP, width)
        back = []
        for i in range(OUT_PARTS):
            some = slice(i * CP // OUT_PARTS, (i + 1) * CP // OUT_PARTS)
            value, slope = gelu_both(pre[some])
            out_ref[some, at] = value.astype(BF)
            out.append(pltpu.make_async_copy(out_ref.at[some, at], out_hbm.at[some, at], out_sem.at[j, i]))
            out[-1].start()
            back.append(cot_ref[some, at].astype(F32) * slope)
        back = jnp.concatenate(back, 0)
        part = dot(t, back.astype(BF), 1, 1)
        product = dot(f[0], planes_of(back, 0).astype(BF), 1, 1)
        for h in range(1, PL // HP):
            product = product + dot(f[h], planes_of(back, h).astype(BF), 1, 1)
        if j == 0:
            acc_ref[...] = part
            product_ref[...] = product
        else:
            acc_ref[...] += part
            product_ref[...] += product
    spectrum = acc_ref[...]
    product = product_ref[...]

    kept = jnp.where(same_plane(PART), product, 0.0)
    kept = jnp.sum(kept.reshape(C, HP, PART), axis=1)
    kept = jnp.concatenate([kept, jnp.zeros((CR - C, PART), F32)], 0)
    hi, lo = split(kept)
    e = channel_of(128)
    y = dot(hi, e, 1, 0) + dot(lo, e, 1, 0)
    yh = y.astype(BF).astype(F32)
    y = yh + pltpu.roll(y - yh, 64, 1)
    extra = y[0:8] + pltpu.roll(y[8:16], C, 1) + pltpu.roll(y[16:24], 2 * C, 1)
    for g in range(groups):
        v = spectrum[g * rows : (g + 1) * rows, :]
        coded = (v * jnp.abs(v)) * (v * v)
        tiles = [coded[:, 128 * i : 128 * (i + 1)] for i in range(CP // 128)]
        o_ref[g] = jnp.concatenate(tiles + [extra], 0).astype(BF)
    for copy in out:
        copy.wait()


def grad_kernel(
    groups, rows, per, r_ref, s_ref, s_rest_ref, pairs_ref, fold_ref, order_ref, o_ref, g_ref, p_ref, g_rest_ref
):
    high = rows * CP // 128
    total = None
    extra = None
    for g in range(groups):
        block = r_ref[g].astype(F32)
        y = root(block[0:high])
        total = y if total is None else total + y
        x = block[high : high + 8]
        extra = x if extra is None else extra + x
    total = total * (1.0 / (SCALE * math.sqrt(MODES)))
    total = jnp.concatenate([total[i * rows : (i + 1) * rows] for i in range(CP // 128)], 1)
    hi, lo = split(total)
    both = jnp.concatenate([hi.astype(F32), lo.astype(F32)], 0).astype(BF)
    hi, lo = split(dot(both, pairs_ref[:, 256:384], 0, 0))
    by_plane = dot(order_ref[...], jnp.concatenate([hi, lo], 1), 1, 0)
    g_ref[...] = by_plane[:, 0:128] + by_plane[:, 128:256]

    rest = per > MAIN
    if rest:
        g_rest_ref[0 : C * 8, :] = across_lanes(dot(both, pairs_ref[:, 384:512], 0, 0))
        g_rest_ref[C * 8 :, :] = jnp.zeros(((CR + 1 - C) * 8, 128), F32)
    for base in range(0, C, 5):
        one = [jnp.zeros((CR, 128), F32)] * 5
        two = [jnp.zeros((CR, 128), F32)] * 5
        for p in range(PL):
            g = g_ref[p * CR : (p + 1) * CR, :]
            for k in range(5):
                row = (base + k) * PL + p
                one[k] = one[k] + s_ref[row : row + 1, :] * g
        for p in range(4 if rest else 0):
            g = g_rest_ref[pl.ds(p, CR, stride=8), :]
            for k in range(5):
                row = (base + k) * 8 + p
                two[k] = two[k] + s_rest_ref[row : row + 1, :] * g
        for k in range(5):
            at = (base + k) * CR
            p_ref[at : at + CR, 0:128] = one[k]
            p_ref[at : at + CR, 128:256] = two[k]
    products = jnp.concatenate([p_ref[c * CR : c * CR + C, :] for c in range(C)], 0)
    hi, lo = split(products)
    both = jnp.concatenate([hi, lo], 1)
    slots = dot(both, fold_ref[...], 1, 0)
    re, im = slots[:, 0:128], slots[:, 128:256]
    lane = lax.broadcasted_iota(jnp.int32, (8, 128), 1)
    extra = extra + pltpu.roll(extra, 64, 1)
    slot = [im[320:], pltpu.roll(im[320:], 128 - C, 1)]
    slot += [extra if k == 0 else pltpu.roll(extra, 128 - k * C, 1) for k in range(3)]
    slot = jnp.concatenate(slot + [jnp.zeros((ROWS - 184, 128), F32)], 0)
    narrow = lax.broadcasted_iota(jnp.int32, (ROWS, 128), 1) < C
    payload = re[0:ROWS] + pltpu.roll(jnp.concatenate([re[ROWS:], im[0:80]], 0), per, 1)
    payload = payload + pltpu.roll(im[80:320], 2 * per, 1)
    o_ref[...] = encode(payload + pltpu.roll(jnp.where(narrow, slot, 0.0), 3 * per, 1))


def last_kernel(per, samples, *refs):
    parts, (grad_ref, mix_ref) = [decode(ref[...]) for ref in refs[:-2]], refs[-2:]
    total = parts[0] + parts[1]
    if len(parts) == 4:
        total = total + (parts[2] + parts[3])
    grads = total * (1.0 / math.sqrt(samples * PL))
    one = pltpu.roll(grads, 128 - per, 1)
    two = pltpu.roll(grads, 128 - 2 * per, 1)
    slot = pltpu.roll(total, 128 - 3 * per, 1)
    grad_ref[0:240, 0, :] = grads[:, 0:per]
    grad_ref[240:400, 0, :] = one[0:160, 0:per]
    grad_ref[0:80, 1, :] = one[160:240, 0:per]
    grad_ref[80:320, 1, :] = two[:, 0:per]
    narrow = lax.broadcasted_iota(jnp.int32, (80, 128), 1) < C
    rest = jnp.where(narrow, slot[0:80], pltpu.roll(slot[80:160], C, 1)) * (1.0 / math.sqrt(samples * PL))
    grad_ref[320:400, 1, :] = rest[:, 0:per]
    mix_ref[...] = slot[160 : 160 + C, 0:C] * (1.0 / math.sqrt(samples * PL * NX * NY))


def sum_over_dp(coded, samples):
    if samples & (samples - 1) or samples == 1:
        total = jnp.sum(decode(lax.all_gather(coded, "dp", axis=0)), axis=0)
        return encode(total), jnp.zeros_like(coded)
    if samples == 4:
        return [coded] + [lax.ppermute(coded, "dp", [(i, i ^ k) for i in range(samples)]) for k in range(1, samples)]
    step = 1
    while True:
        other = lax.ppermute(coded, "dp", [(i, i ^ step) for i in range(samples)])
        step *= 2
        if step >= samples:
            return coded, other
        coded = encode(decode(coded) + decode(other))


def compiler_params(mib):
    return pltpu.CompilerParams(vmem_limit_bytes=mib * 2**20)


def local(tables, consts, fields, cotangent, mix_weight, spectral_weight):
    wsel, collect, fold, pairs = consts
    cells = fields.shape[3]
    groups = lax.axis_size("gx") * lax.axis_size("gy")
    samples = lax.axis_size("dp")
    per = MODES // groups
    rows = round_up(2 * per, 8)
    flat = fields.reshape(CP, cells)
    cot = cotangent.reshape(CP, cells)
    gid = (lax.axis_index("gx") * lax.axis_size("gy") + lax.axis_index("gy")).astype(jnp.int32).reshape(1)
    halves = max(1, cells // 1024)
    high = groups * rows
    vmem = pl.BlockSpec(memory_space=pltpu.VMEM)
    smem = pl.BlockSpec(memory_space=pltpu.SMEM)

    hbm = pl.BlockSpec(memory_space=pltpu.HBM)

    sent, flat_in, table_in = pl.pallas_call(
        functools.partial(first_kernel, groups, rows, halves),
        in_specs=[smem, hbm, hbm],
        out_specs=(vmem, vmem, vmem),
        out_shape=(
            jax.ShapeDtypeStruct((groups, rows, CP), BF),
            jax.ShapeDtypeStruct((CP, cells), BF),
            jax.ShapeDtypeStruct((high, cells), BF),
        ),
        scratch_shapes=[
            pltpu.VMEM((high, CP), F32),
            pltpu.SemaphoreType.DMA((2, halves)),
        ],
        compiler_params=compiler_params(50),
        name="spectrum_parts",
    )(gid, flat, tables)
    got = lax.all_to_all(sent, GROUP, 0, 0, tiled=True)

    weights = jnp.transpose(spectral_weight, (2, 3, 1, 0)).reshape(C * C, 2, per)
    vals, spec, spec_rest, cot_in = pl.pallas_call(
        functools.partial(mix_kernel, groups, rows, per),
        in_specs=[hbm] + [vmem] * 5,
        out_specs=[vmem] * 4,
        out_shape=[
            jax.ShapeDtypeStruct((rows, CP), BF),
            jax.ShapeDtypeStruct((CP, 128), F32),
            jax.ShapeDtypeStruct((C * 8, 128), F32),
            jax.ShapeDtypeStruct((CP, cells), BF),
        ],
        scratch_shapes=[
            pltpu.VMEM((C * C, 256), F32),
            pltpu.VMEM((CP, 128), F32),
            pltpu.VMEM((C * 8, 128), F32),
            pltpu.SemaphoreType.DMA((1,)),
        ],
        compiler_params=compiler_params(48),
        name="mode_mixing",
    )(cot, got, weights, wsel, collect, pairs)
    all_vals = lax.all_gather(vals, GROUP, axis=0, tiled=True)

    output, sent = pl.pallas_call(
        functools.partial(main_kernel, groups, rows, 1),
        in_specs=[vmem] * 5,
        out_specs=(hbm, vmem),
        out_shape=(
            jax.ShapeDtypeStruct((CP, cells), BF),
            jax.ShapeDtypeStruct((groups, rows * CP // 128 + 8, 128), BF),
        ),
        scratch_shapes=[
            pltpu.VMEM((CP, cells), BF),
            pltpu.VMEM((PL // HP, PART, high + PART), BF),
            pltpu.VMEM((high, CP), F32),
            pltpu.VMEM((PART, PART), F32),
            pltpu.SemaphoreType.DMA((1, OUT_PARTS)),
        ],
        compiler_params=compiler_params(40),
        name="cells",
    )(table_in, flat_in, cot_in, all_vals, mix_weight)
    got = lax.all_to_all(sent, GROUP, 0, 0, tiled=True)

    coded = pl.pallas_call(
        functools.partial(grad_kernel, groups, rows, per),
        out_shape=jax.ShapeDtypeStruct((ROWS, 128), BF),
        scratch_shapes=[pltpu.VMEM((CR * PL, 128), F32), pltpu.VMEM((C * CR, 256), F32), pltpu.VMEM(((CR + 1) * 8, 128), F32)],
        compiler_params=compiler_params(8),
        name="mode_grads",
    )(got, spec, spec_rest, pairs, fold, plane_order())
    summands = sum_over_dp(coded, samples)
    grads, mixing_grad = pl.pallas_call(
        functools.partial(last_kernel, per, samples),
        out_shape=(jax.ShapeDtypeStruct((C * C, 2, per), F32), jax.ShapeDtypeStruct((C, C), F32)),
        compiler_params=compiler_params(8),
        name="gradients_out",
    )(*summands)
    spectral_grad = jnp.transpose(grads.reshape(C, C, 2, per), (3, 2, 0, 1))
    return (output.reshape(1, C, PL, cells), spectral_grad, mixing_grad)


def solution(mesh):
    groups = mesh.shape["gx"] * mesh.shape["gy"]
    body = functools.partial(local, table(groups), selectors(groups))
    return jax.shard_map(
        body,
        mesh=mesh,
        in_specs=(
            P("dp", None, None, GROUP),
            P("dp", None, None, GROUP),
            P(),
            P(GROUP, None, None, None),
        ),
        out_specs=(P("dp", None, None, GROUP), P(GROUP, None, None, None), P()),
        check_vma=False,
    )
```

```python
import functools
import math

import jax
import jax.numpy as jnp
import ml_dtypes
import numpy as np
from jax import lax
from jax.experimental import pallas as pl
from jax.experimental.pallas import tpu as pltpu
from jax.sharding import PartitionSpec as P

NX = 128
NY = 128
KX = 24
KY = 12
MODES = 288
C = 20
PL = 32
CP = C * PL
HP = 8
PART = C * HP
OUT_PARTS = 4
MAIN = 32
ROWS = 240
CR = 24
SCALE = 1.6656925
GROUP = ("gx", "gy")
BF = jnp.bfloat16
F32 = jnp.float32


def round_up(n, k):
    return -(-n // k) * k


def table(groups):
    per = MODES // groups
    rows = round_up(2 * per, 8)
    index = np.arange(KX)
    waves_x = np.where(index < KX // 2, index, NX - KX + index)
    kx = np.repeat(waves_x, KY)
    ky = np.tile(np.arange(KY), KX)
    x = np.arange(NX * NY) // NY
    y = np.arange(NX * NY) % NY
    turn = (kx[:, None] * x[None] + ky[:, None] * y[None]) % 128
    wheel = 2.0 * np.pi * np.arange(128) / 128
    both = np.stack([(SCALE * np.cos(wheel))[turn], (-SCALE * np.sin(wheel))[turn]], 0)
    both = both.reshape(2, groups, per, -1).transpose(1, 0, 2, 3).reshape(groups, 2 * per, -1)
    full = np.zeros((groups, rows, NX * NY), np.float32)
    full[:, : 2 * per] = both
    full = full.reshape(groups * rows, groups, -1).transpose(1, 0, 2)
    return full.astype(ml_dtypes.bfloat16)


def selectors(groups):
    per = MODES // groups
    rows = round_up(2 * per, 8)
    re, im = np.arange(per), per + np.arange(per)
    main = min(per, MAIN)
    pairs = np.zeros((rows, 512), np.float32)
    weights = np.zeros((2, per, 256), np.float32)
    collect = np.zeros((rows, 256), np.float32)
    fold = np.zeros((256, 256), np.float32)
    for k, (s_row, s_sign, g_row) in enumerate(((re, 1, re), (im, 1, im), (im, -1, re), (re, 1, im))):
        for m in range(per):
            places = [k * MAIN + m] if m < main else [128 + 16 * j + 4 * k + m - main for j in range(8)]
            for at in places:
                pairs[s_row[m], at] = s_sign
                pairs[g_row[m], 256 + at] = 1
                fold[at, 128 * (k // 2) + m] = 1
                weights[k // 2, m, at] = 1
                collect[(re, im)[k % 2][m], at] = 1
    cast = lambda a: a.astype(ml_dtypes.bfloat16)
    return (
        cast(weights),
        cast(np.concatenate([collect, collect], 1)),
        cast(np.concatenate([fold, fold], 0)),
        cast(np.concatenate([pairs, pairs], 0)),
    )


def plane_order():
    order = np.zeros((PL, CR, C, PL), np.float32)
    for d in range(C):
        order[np.arange(PL), d, d, np.arange(PL)] = 1
    return order.reshape(PL * CR, CP).astype(ml_dtypes.bfloat16)


def dot(a, b, ca, cb):
    return lax.dot_general(a, b, (((ca,), (cb,)), ((), ())), preferred_element_type=F32)


def squared(v):
    return v * jnp.abs(v)


def square_root(y):
    y = y.astype(F32)
    return y * lax.rsqrt(jnp.maximum(jnp.abs(y), 1e-36))


def encode(v):
    return ((v * jnp.abs(v)) * (v * v)).astype(BF)


def decode(y):
    return root(y.astype(F32))


def root(y):
    z = lax.rsqrt(jnp.maximum(jnp.abs(y), 1e-36))
    return ((y * z) * z) * lax.rsqrt(z)


def split(v):
    hi = v.astype(BF)
    return hi, (v - hi.astype(F32)).astype(BF)


def chunk_copies(pairs, parts, sem):
    copies = []
    for j in range(parts):
        copies.append([])
        for k, (source, target) in enumerate(pairs):
            width = target.shape[-1] // parts
            index = (slice(None),) * (len(target.shape) - 1) + (pl.ds(j * width, width),)
            copies[j].append(pltpu.make_async_copy(source.at[index], target.at[index], sem.at[k, j]))
    return copies


def start_chunk(copies, j):
    if j < len(copies):
        for copy in copies[j]:
            copy.start()


def first_kernel(groups, rows, parts, gid_ref, f_hbm, t_hbm, o_ref, f_ref, t_ref, acc_ref, sem):
    gid = gid_ref[0]
    width = f_ref.shape[1] // parts
    copies = chunk_copies([(f_hbm, f_ref), (t_hbm.at[gid], t_ref)], parts, sem)
    for j in range(parts):
        start_chunk(copies, j)
    for j in range(parts):
        at = slice(j * width, (j + 1) * width)
        for copy in copies[j]:
            copy.wait()
        part = dot(t_ref[:, at], f_ref[:, at], 1, 1)
        if j == 0:
            acc_ref[...] = part
        elif j < parts - 1:
            acc_ref[...] += part
    sent = acc_ref[...] + part if parts > 1 else part
    for g in range(groups):
        o_ref[g] = squared(sent[g * rows : (g + 1) * rows, :]).astype(BF)


def same_plane(n):
    i = lax.broadcasted_iota(jnp.int32, (n, n), 0)
    j = lax.broadcasted_iota(jnp.int32, (n, n), 1)
    return lax.rem(i, HP) == lax.rem(j, HP)


def channel_of(lanes):
    i = lax.broadcasted_iota(jnp.int32, (PART, lanes), 0)
    j = lax.broadcasted_iota(jnp.int32, (PART, lanes), 1)
    return jnp.where(lax.div(i, HP) == j, 1.0, 0.0).astype(BF)


def planes_of(x, h):
    return x.reshape(C, PL // HP, HP, x.shape[1])[:, h].reshape(PART, x.shape[1])


def own_group():
    shape = (PL // 8, 8, 128)
    group = 2 * lax.broadcasted_iota(jnp.int32, shape, 0) + lax.div(lax.broadcasted_iota(jnp.int32, shape, 1), 4)
    return group == lax.div(lax.broadcasted_iota(jnp.int32, shape, 2), 16)


def across_lanes(x):
    x = jnp.where(own_group()[None], x.reshape(C, PL // 8, 8, 128), 0.0)
    x = jnp.sum(x, axis=1)
    return (x + jnp.concatenate([x[:, 4:], x[:, :4]], 1)).reshape(C * 8, 128)


def along_planes(x):
    return jnp.where(own_group()[None], x.reshape(C, 1, 8, 128), 0.0).reshape(CP, 128)


def mix_kernel(
    groups, rows, per, cot_hbm, r_ref, w_ref, wsel_ref, collect_ref, pairs_ref,
    v_ref, spec_ref, spec_rest_ref, cot_ref, weights_ref, vals_ref, rest_ref, sem,
):
    cot_copy = pltpu.make_async_copy(cot_hbm, cot_ref, sem.at[0])
    cot_copy.start()
    total = square_root(r_ref[0])
    for g in range(1, groups):
        total = total + square_root(r_ref[g])
    total = total * (1.0 / (SCALE * math.sqrt(NX * NY)))
    hi, lo = split(total)
    both = jnp.concatenate([hi.astype(F32), lo.astype(F32)], 0).astype(BF)
    spec_ref[...] = dot(both, pairs_ref[:, 0:128], 0, 0)
    spec_rest_ref[...] = across_lanes(dot(both, pairs_ref[:, 128:256], 0, 0))
    w = w_ref[...].astype(F32)
    weights_ref[...] = dot(w[:, 0, :].astype(BF), wsel_ref[0], 1, 0) + dot(w[:, 1, :].astype(BF), wsel_ref[1], 1, 0)

    for base in range(0, C, 4):
        main = [None] * 4
        rest = [None] * 4
        for c in range(C):
            s = spec_ref[c * PL : (c + 1) * PL, :]
            t = spec_rest_ref[c * 8 : (c + 1) * 8, :]
            for k in range(4):
                row = c * C + base + k
                one = s * weights_ref[row : row + 1, 0:128]
                main[k] = one if main[k] is None else main[k] + one
                two = t * weights_ref[row : row + 1, 128:256]
                rest[k] = two if rest[k] is None else rest[k] + two
        for k in range(4):
            d = base + k
            vals_ref[d * PL : (d + 1) * PL, :] = main[k]
            rest_ref[d * 8 : (d + 1) * 8, :] = rest[k]
    vals = jnp.concatenate([vals_ref[...], along_planes(rest_ref[...])], 1)
    hi, lo = split(vals * (1.0 / (SCALE * math.sqrt(MODES))))
    v_ref[...] = dot(collect_ref[...], jnp.concatenate([hi, lo], 1), 1, 1).astype(BF)
    cot_copy.wait()


def gelu_both(h):
    k = math.sqrt(2.0 / math.pi)
    h2 = h * h
    t = jnp.tanh(h * (k + (k * 0.044715) * h2))
    half = 0.5 + 0.5 * t
    slope = half + (h * (half * (1.0 - t))) * (k + (3.0 * 0.044715 * k) * h2)
    return h * half, slope


def main_kernel(
    groups, rows, parts, t_ref, f_ref, cot_ref, v_ref, mix_ref, out_hbm, o_ref,
    out_ref, a_ref, acc_ref, product_ref, out_sem,
):
    width = f_ref.shape[1] // parts
    vals = jnp.transpose(v_ref[...].astype(F32))
    e = channel_of(C)
    m = jnp.where(same_plane(PART), dot(dot(e, mix_ref[...], 1, 1).astype(BF), e, 1, 1), 0.0)
    for h in range(PL // HP):
        a_ref[h] = jnp.concatenate([planes_of(vals, h), m], 1).astype(BF)
    out = []
    for j in range(parts):
        at = slice(j * width, (j + 1) * width)
        t = t_ref[:, at]
        f = f_ref[:, at].astype(F32)
        f = [planes_of(f, h).astype(BF) for h in range(PL // HP)]
        pre = [dot(a_ref[h], jnp.concatenate([t, f[h]], 0), 1, 0) for h in range(PL // HP)]
        pre = jnp.stack([x.reshape(C, HP, width) for x in pre], 1).reshape(CP, width)
        back = []
        for i in range(OUT_PARTS):
            some = slice(i * CP // OUT_PARTS, (i + 1) * CP // OUT_PARTS)
            value, slope = gelu_both(pre[some])
            out_ref[some, at] = value.astype(BF)
            out.append(pltpu.make_async_copy(out_ref.at[some, at], out_hbm.at[some, at], out_sem.at[j, i]))
            out[-1].start()
            back.append(cot_ref[some, at].astype(F32) * slope)
        back = jnp.concatenate(back, 0)
        part = dot(t, back.astype(BF), 1, 1)
        product = dot(f[0], planes_of(back, 0).astype(BF), 1, 1)
        for h in range(1, PL // HP):
            product = product + dot(f[h], planes_of(back, h).astype(BF), 1, 1)
        if j == 0:
            acc_ref[...] = part
            product_ref[...] = product
        else:
            acc_ref[...] += part
            product_ref[...] += product
    spectrum = acc_ref[...]
    product = product_ref[...]

    kept = jnp.where(same_plane(PART), product, 0.0)
    kept = jnp.sum(kept.reshape(C, HP, PART), axis=1)
    kept = jnp.concatenate([kept, jnp.zeros((CR - C, PART), F32)], 0)
    hi, lo = split(kept)
    e = channel_of(128)
    y = dot(hi, e, 1, 0) + dot(lo, e, 1, 0)
    yh = y.astype(BF).astype(F32)
    y = yh + pltpu.roll(y - yh, 64, 1)
    extra = y[0:8] + pltpu.roll(y[8:16], C, 1) + pltpu.roll(y[16:24], 2 * C, 1)
    for g in range(groups):
        v = spectrum[g * rows : (g + 1) * rows, :]
        coded = squared(v)
        tiles = [coded[:, 128 * i : 128 * (i + 1)] for i in range(CP // 128)]
        o_ref[g] = jnp.concatenate(tiles + [extra], 0).astype(BF)
    for copy in out:
        copy.wait()


def grad_kernel(
    groups, rows, per, r_ref, s_ref, s_rest_ref, pairs_ref, fold_ref, order_ref, o_ref, g_ref, p_ref, g_rest_ref
):
    high = rows * CP // 128
    total = None
    extra = None
    for g in range(groups):
        block = r_ref[g].astype(F32)
        y = square_root(block[0:high])
        total = y if total is None else total + y
        x = block[high : high + 8]
        extra = x if extra is None else extra + x
    total = total * (1.0 / (SCALE * math.sqrt(MODES)))
    total = jnp.concatenate([total[i * rows : (i + 1) * rows] for i in range(CP // 128)], 1)
    hi, lo = split(total)
    both = jnp.concatenate([hi.astype(F32), lo.astype(F32)], 0).astype(BF)
    hi, lo = split(dot(both, pairs_ref[:, 256:384], 0, 0))
    by_plane = dot(order_ref[...], jnp.concatenate([hi, lo], 1), 1, 0)
    g_ref[...] = by_plane[:, 0:128] + by_plane[:, 128:256]

    rest = per > MAIN
    if rest:
        g_rest_ref[0 : C * 8, :] = across_lanes(dot(both, pairs_ref[:, 384:512], 0, 0))
        g_rest_ref[C * 8 :, :] = jnp.zeros(((CR + 1 - C) * 8, 128), F32)
    for base in range(0, C, 5):
        one = [jnp.zeros((CR, 128), F32)] * 5
        two = [jnp.zeros((CR, 128), F32)] * 5
        for p in range(PL):
            g = g_ref[p * CR : (p + 1) * CR, :]
            for k in range(5):
                row = (base + k) * PL + p
                one[k] = one[k] + s_ref[row : row + 1, :] * g
        for p in range(4 if rest else 0):
            g = g_rest_ref[pl.ds(p, CR, stride=8), :]
            for k in range(5):
                row = (base + k) * 8 + p
                two[k] = two[k] + s_rest_ref[row : row + 1, :] * g
        for k in range(5):
            at = (base + k) * CR
            p_ref[at : at + CR, 0:128] = one[k]
            p_ref[at : at + CR, 128:256] = two[k]
    products = jnp.concatenate([p_ref[c * CR : c * CR + C, :] for c in range(C)], 0)
    hi, lo = split(products)
    both = jnp.concatenate([hi, lo], 1)
    slots = dot(both, fold_ref[...], 1, 0)
    re, im = slots[:, 0:128], slots[:, 128:256]
    lane = lax.broadcasted_iota(jnp.int32, (8, 128), 1)
    extra = extra + pltpu.roll(extra, 64, 1)
    slot = [im[320:], pltpu.roll(im[320:], 128 - C, 1)]
    slot += [extra if k == 0 else pltpu.roll(extra, 128 - k * C, 1) for k in range(3)]
    slot = jnp.concatenate(slot + [jnp.zeros((ROWS - 184, 128), F32)], 0)
    narrow = lax.broadcasted_iota(jnp.int32, (ROWS, 128), 1) < C
    payload = re[0:ROWS] + pltpu.roll(jnp.concatenate([re[ROWS:], im[0:80]], 0), per, 1)
    payload = payload + pltpu.roll(im[80:320], 2 * per, 1)
    o_ref[...] = encode(payload + pltpu.roll(jnp.where(narrow, slot, 0.0), 3 * per, 1))


def last_kernel(per, samples, *refs):
    parts, (grad_ref, mix_ref) = [decode(ref[...]) for ref in refs[:-2]], refs[-2:]
    total = parts[0] + parts[1]
    if len(parts) == 4:
        total = total + (parts[2] + parts[3])
    grads = total * (1.0 / math.sqrt(samples * PL))
    one = pltpu.roll(grads, 128 - per, 1)
    two = pltpu.roll(grads, 128 - 2 * per, 1)
    slot = pltpu.roll(total, 128 - 3 * per, 1)
    grad_ref[0:240, 0, :] = grads[:, 0:per]
    grad_ref[240:400, 0, :] = one[0:160, 0:per]
    grad_ref[0:80, 1, :] = one[160:240, 0:per]
    grad_ref[80:320, 1, :] = two[:, 0:per]
    narrow = lax.broadcasted_iota(jnp.int32, (80, 128), 1) < C
    rest = jnp.where(narrow, slot[0:80], pltpu.roll(slot[80:160], C, 1)) * (1.0 / math.sqrt(samples * PL))
    grad_ref[320:400, 1, :] = rest[:, 0:per]
    mix_ref[...] = slot[160 : 160 + C, 0:C] * (1.0 / math.sqrt(samples * PL * NX * NY))


def sum_over_dp(coded, samples):
    if samples & (samples - 1) or samples == 1:
        total = jnp.sum(decode(lax.all_gather(coded, "dp", axis=0)), axis=0)
        return encode(total), jnp.zeros_like(coded)
    if samples == 4:
        return [coded] + [lax.ppermute(coded, "dp", [(i, i ^ k) for i in range(samples)]) for k in range(1, samples)]
    step = 1
    while True:
        other = lax.ppermute(coded, "dp", [(i, i ^ step) for i in range(samples)])
        step *= 2
        if step >= samples:
            return coded, other
        coded = encode(decode(coded) + decode(other))


def compiler_params(mib):
    return pltpu.CompilerParams(vmem_limit_bytes=mib * 2**20)


def local(tables, consts, fields, cotangent, mix_weight, spectral_weight):
    wsel, collect, fold, pairs = consts
    cells = fields.shape[3]
    groups = lax.axis_size("gx") * lax.axis_size("gy")
    samples = lax.axis_size("dp")
    per = MODES // groups
    rows = round_up(2 * per, 8)
    flat = fields.reshape(CP, cells)
    cot = cotangent.reshape(CP, cells)
    gid = (lax.axis_index("gx") * lax.axis_size("gy") + lax.axis_index("gy")).astype(jnp.int32).reshape(1)
    halves = max(1, cells // 1024)
    high = groups * rows
    vmem = pl.BlockSpec(memory_space=pltpu.VMEM)
    smem = pl.BlockSpec(memory_space=pltpu.SMEM)

    hbm = pl.BlockSpec(memory_space=pltpu.HBM)

    sent, flat_in, table_in = pl.pallas_call(
        functools.partial(first_kernel, groups, rows, halves),
        in_specs=[smem, hbm, hbm],
        out_specs=(vmem, vmem, vmem),
        out_shape=(
            jax.ShapeDtypeStruct((groups, rows, CP), BF),
            jax.ShapeDtypeStruct((CP, cells), BF),
            jax.ShapeDtypeStruct((high, cells), BF),
        ),
        scratch_shapes=[
            pltpu.VMEM((high, CP), F32),
            pltpu.SemaphoreType.DMA((2, halves)),
        ],
        compiler_params=compiler_params(50),
        name="spectrum_parts",
    )(gid, flat, tables)
    got = lax.all_to_all(sent, GROUP, 0, 0, tiled=True)

    weights = jnp.transpose(spectral_weight, (2, 3, 1, 0)).reshape(C * C, 2, per)
    vals, spec, spec_rest, cot_in = pl.pallas_call(
        functools.partial(mix_kernel, groups, rows, per),
        in_specs=[hbm] + [vmem] * 5,
        out_specs=[vmem] * 4,
        out_shape=[
            jax.ShapeDtypeStruct((rows, CP), BF),
            jax.ShapeDtypeStruct((CP, 128), F32),
            jax.ShapeDtypeStruct((C * 8, 128), F32),
            jax.ShapeDtypeStruct((CP, cells), BF),
        ],
        scratch_shapes=[
            pltpu.VMEM((C * C, 256), F32),
            pltpu.VMEM((CP, 128), F32),
            pltpu.VMEM((C * 8, 128), F32),
            pltpu.SemaphoreType.DMA((1,)),
        ],
        compiler_params=compiler_params(48),
        name="mode_mixing",
    )(cot, got, weights, wsel, collect, pairs)
    all_vals = lax.all_gather(vals, GROUP, axis=0, tiled=True)

    output, sent = pl.pallas_call(
        functools.partial(main_kernel, groups, rows, 1),
        in_specs=[vmem] * 5,
        out_specs=(hbm, vmem),
        out_shape=(
            jax.ShapeDtypeStruct((CP, cells), BF),
            jax.ShapeDtypeStruct((groups, rows * CP // 128 + 8, 128), BF),
        ),
        scratch_shapes=[
            pltpu.VMEM((CP, cells), BF),
            pltpu.VMEM((PL // HP, PART, high + PART), BF),
            pltpu.VMEM((high, CP), F32),
            pltpu.VMEM((PART, PART), F32),
            pltpu.SemaphoreType.DMA((1, OUT_PARTS)),
        ],
        compiler_params=compiler_params(40),
        name="cells",
    )(table_in, flat_in, cot_in, all_vals, mix_weight)
    got = lax.all_to_all(sent, GROUP, 0, 0, tiled=True)

    coded = pl.pallas_call(
        functools.partial(grad_kernel, groups, rows, per),
        out_shape=jax.ShapeDtypeStruct((ROWS, 128), BF),
        scratch_shapes=[pltpu.VMEM((CR * PL, 128), F32), pltpu.VMEM((C * CR, 256), F32), pltpu.VMEM(((CR + 1) * 8, 128), F32)],
        compiler_params=compiler_params(8),
        name="mode_grads",
    )(got, spec, spec_rest, pairs, fold, plane_order())
    summands = sum_over_dp(coded, samples)
    grads, mixing_grad = pl.pallas_call(
        functools.partial(last_kernel, per, samples),
        out_shape=(jax.ShapeDtypeStruct((C * C, 2, per), F32), jax.ShapeDtypeStruct((C, C), F32)),
        compiler_params=compiler_params(8),
        name="gradients_out",
    )(*summands)
    spectral_grad = jnp.transpose(grads.reshape(C, C, 2, per), (3, 2, 0, 1))
    return (output.reshape(1, C, PL, cells), spectral_grad, mixing_grad)


def solution(mesh):
    groups = mesh.shape["gx"] * mesh.shape["gy"]
    body = functools.partial(local, table(groups), selectors(groups))
    return jax.shard_map(
        body,
        mesh=mesh,
        in_specs=(
            P("dp", None, None, GROUP),
            P("dp", None, None, GROUP),
            P(),
            P(GROUP, None, None, None),
        ),
        out_specs=(P("dp", None, None, GROUP), P(GROUP, None, None, None), P()),
        check_vma=False,
    )
```
